32 devices in a mesh: band: 2 (over y), lon: 16 (over z, x, core).
Axes of the slice: x: 2, y: 2, z: 4, core: 2. Of those that a mesh axis runs over, the one named last changes fastest.
Arguments:
- tracers: float32 [96, 256, 128], P('band', 'lon'), may hold values from -6 to 6
- lon_offset: int32 [96, 4], P('band'), may hold values from -128 to 127
- lon_weights: float32 [4, 96, 4], P(None, 'band'), may hold values from -0.1 to 1, as said below
- lat_offset: int32 [96, 4], P('band'), may hold values from -6 to 6
- lat_weights: float32 [4, 96, 4], P(None, 'band'), may hold values from -0.1 to 1, as said below
Outputs:
- advected: float32 [96, 256, 128], P('band', 'lon')
The draws below stay inside these ranges and needn't reach their ends.
Inputs may be any that keep to these rules, and one draw needn't show every extreme that they name: `lon_weights`: each set of four weights sums to one. `lat_weights`: each set of four weights sums to one.
All inputs are finite; a program needn't handle non-finite values.
Results may differ from the reference program's by a relative error of at most 0.0003.
Values sent between devices are 32-bit elements; how exact they have to be, the bound alone decides.
A program may use at most 64 MiB of HBM per device.

```python
import jax
import jax.numpy as jnp
from jax import lax

LEV = 4
TRACERS = 32
TMAX = 6
NLAT = 96
NLON = 256
COLS = 128


def cubic_table(key):
    frac = jax.random.uniform(key, (NLAT, LEV), jnp.float32)
    left = -frac * (1.0 - frac) * (2.0 - frac) / 6.0
    centre = (1.0 + frac) * (1.0 - frac) * (2.0 - frac) / 2.0
    right = (1.0 + frac) * frac * (2.0 - frac) / 2.0
    outer = -(1.0 + frac) * frac * (1.0 - frac) / 6.0
    return jnp.stack([left, centre, right, outer]).astype(jnp.float32)


def draw_lon_weights(key, part):
    return cubic_table(jax.random.fold_in(key, 11))


def draw_lat_weights(key, part):
    return cubic_table(jax.random.fold_in(key, 12))


def draw_lon_offset(key, part):
    rows = jnp.arange(NLAT, dtype=jnp.int32)
    dist = jnp.abs(2 * rows - (NLAT - 1))
    reach = 2 + (NLON // 2 - 2) * dist * dist // ((NLAT - 1) * (NLAT - 1))
    values = jax.random.randint(jax.random.fold_in(key, 13), (NLAT, LEV), -reach[:, None], reach[:, None] + 1, dtype=jnp.int32)
    values = jnp.minimum(values, NLON // 2 - 1)
    values = values.at[0, 0].set(NLON // 2 - 1)
    values = values.at[NLAT - 1, 0].set(-(NLON // 2))
    return values


def with_ends(entries, rng, smallest, high):
    index_at = [jax.random.randint(jax.random.fold_in(rng, axis), (), 0, length) for axis, length in enumerate(entries.shape)]
    main_axis = entries.shape.index(max(entries.shape))
    beside = index_at[:main_axis] + [(index_at[main_axis] + 1) % entries.shape[main_axis]] + index_at[main_axis + 1:]
    return entries.at[tuple(index_at)].set(smallest).at[tuple(beside)].set(high)


def steps_of(own_key, shape, cuts, least, high):
    factor_of, own = 1.0, jax.random.fold_in(own_key, 6)
    for dim, shards_of in cuts:
        steps = jnp.exp(jax.random.uniform(jax.random.fold_in(own, dim), (shards_of,), jnp.float32, least / len(cuts), high / len(cuts)))
        factor_of = factor_of * jnp.repeat(steps, shape[dim] // shards_of).reshape([-1 if axis == dim else 1 for axis in range(len(shape))])
    return factor_of


def bell_draw(key, extent, width, most, cuts=(), kind=jnp.bfloat16):
    array = jax.random.normal(key, extent, jnp.float32) * width
    if len(cuts) > 0:
        array = steps_of(key, extent, cuts, -0.22, 0.18) * array
    return jnp.clip(array, min=-most, max=most).astype(kind)


def setup_inputs(seed: int = 0) -> dict:
    streams_of = jax.random.split(jax.random.key(seed), 6)
    return {
        "tracers": bell_draw(streams_of[0], (NLAT, NLON, COLS), 1.0, 6.0, ((0, 2), (1, 16)), jnp.float32),
        "lon_offset": draw_lon_offset(jax.random.fold_in(streams_of[5], 71), 0),
        "lon_weights": draw_lon_weights(jax.random.fold_in(streams_of[5], 71), 0),
        "lat_offset": with_ends(jax.random.randint(streams_of[3], (NLAT, LEV), -TMAX, TMAX + 1), jax.random.fold_in(streams_of[3], 1), -TMAX, TMAX).astype(jnp.int32),
        "lat_weights": draw_lat_weights(jax.random.fold_in(streams_of[5], 71), 0),
    }


def zonal_pass(field, offsets, weights):
    cells = jnp.arange(NLON, dtype=jnp.int32)
    rows = jnp.arange(NLAT, dtype=jnp.int32)

    def one_level(packed):
        plane, shifts, coeffs = packed
        total = jnp.zeros_like(plane)
        for k in range(4):
            index = jnp.mod(cells[None, :] - shifts[:, None] + (k - 1), NLON).astype(jnp.int32)
            total = total + coeffs[k][:, None, None] * plane[rows[:, None], index]
        return total

    result = lax.map(one_level, (field.transpose(2, 0, 1, 3), offsets.T, weights.transpose(2, 0, 1)))
    return result.transpose(1, 2, 0, 3)


def meridional_pass(field, offsets, weights):
    rows = jnp.arange(NLAT, dtype=jnp.int32)

    def one_level(packed):
        plane, shifts, coeffs = packed
        total = jnp.zeros_like(plane)
        for k in range(4):
            source = jnp.clip(rows - shifts + (k - 1), 0, NLAT - 1).astype(jnp.int32)
            total = total + coeffs[k][:, None, None] * plane[source]
        return total

    result = lax.map(one_level, (field.transpose(2, 0, 1, 3), offsets.T, weights.transpose(2, 0, 1)))
    return result.transpose(1, 2, 0, 3)


def reference(tracers, lon_offset, lon_weights, lat_offset, lat_weights):
    field = tracers.reshape(NLAT, NLON, LEV, TRACERS)
    first = zonal_pass(field, lon_offset, lon_weights)
    second = meridional_pass(first, lat_offset, lat_weights)
    third = zonal_pass(second, lon_offset, lon_weights)
    return third.reshape(NLAT, NLON, LEV * TRACERS)
```

```python
import functools
import math

import jax
import jax.numpy as jnp
from jax import lax
from jax.experimental import pallas as pl
from jax.experimental.pallas import tpu as pltpu
from jax.sharding import PartitionSpec as P

TMAX = 6
REACH = TMAX + 2
SUB = 8
PIECE = 16


def turned(parts, per):
    parts = list(parts)
    count = len(parts)
    lanes = parts[0].shape[1]
    block = lax.broadcasted_iota(jnp.int32, parts[0].shape, 1) // per
    bit = count // 2
    while bit:
        high = (block // bit) % 2 == 1
        move = per * bit
        for i in range(count):
            if i & bit:
                continue
            a, b = parts[i], parts[i | bit]
            parts[i] = jnp.where(high, pltpu.roll(b, move, 1), a)
            parts[i | bit] = jnp.where(high, b, pltpu.roll(a, lanes - move, 1))
        bit //= 2
    return parts


def circled(field, offset, weights, per):
    count, lanes = field.shape
    lane = lax.broadcasted_iota(jnp.int32, field.shape, 1)
    following = pltpu.roll(field, count - 1, 0)
    total = weights[0] * field
    for k in range(1, 4):
        mixed = jnp.where(lane >= per * k, field, following)
        total = total + weights[k] * pltpu.roll(mixed, lanes - per * k, 1)
    shift = ((offset + 1) * per + count * lanes) % (count * lanes)
    coarse, fine = shift // lanes, shift % lanes
    near = pltpu.roll(total, coarse, 0)
    far = pltpu.roll(near, 1, 0)
    return pltpu.roll(jnp.where(lane < lanes - fine, near, far), fine, 1)


def kernel(
    n, bands, groups, rows, piece, per, per_level,
    x_ref, lon_off, lon_w, lat_off, lat_w, out_ref,
    send, recv, first, back, home,
    send_sem, recv_sem, back_sem, home_sem, halo_send, halo_recv, own_sem,
):
    me = lax.axis_index("lon")
    split = n // groups
    group, share = me // split, me % split
    part = lax.axis_index("band") * split + share
    parts_all = bands * split
    level = group * per // per_level
    chunks = rows // piece
    tile_rows = math.gcd(SUB, piece)
    slot = send.shape[0] // n
    order = [0, chunks - 1] + list(range(1, chunks - 1)) if chunks > 1 else [0]

    barrier = pltpu.get_barrier_semaphore()

    def greet(d, carry):
        pl.semaphore_signal(
            barrier, inc=1, device_id={"lon": lax.rem(me + d, n)},
            device_id_type=pl.DeviceIdType.MESH,
        )
        return carry

    lax.fori_loop(1, n, greet, 0)

    def beside(step):
        other = lax.rem(part + step + parts_all, parts_all)
        return {"band": other // split, "lon": group * split + other % split}

    @pl.when(part > 0)
    def _():
        pl.semaphore_signal(
            barrier, inc=1, device_id=beside(-1), device_id_type=pl.DeviceIdType.MESH
        )

    @pl.when(part < parts_all - 1)
    def _():
        pl.semaphore_signal(
            barrier, inc=1, device_id=beside(1), device_id_type=pl.DeviceIdType.MESH
        )

    def place_of(peer, chunk):
        return pl.ds(pl.multiple_of(peer * slot + chunk * piece, SUB), piece)

    def pack(chunk):
        for s in range(split):

            def tile(t, carry):
                row = chunk * piece + t * tile_rows
                start = (s * rows + row) * groups
                parts = [
                    x_ref[pl.ds(start + i, tile_rows, stride=groups), :] for i in range(groups)
                ]
                for g, block in enumerate(turned(parts, per)):
                    to = (g * split + s) * slot + row
                    send[pl.ds(pl.multiple_of(to, tile_rows), tile_rows), :] = block
                return carry

            lax.fori_loop(0, piece // tile_rows, tile, 0)

    def across(source, target, s_sem, r_sem, chunk, d):
        peer = lax.rem(me + d, n)
        return pltpu.make_async_remote_copy(
            src_ref=source.at[place_of(peer, chunk), :],
            dst_ref=target.at[place_of(me, chunk), :],
            send_sem=s_sem.at[chunk, d],
            recv_sem=r_sem.at[chunk, d],
            device_id={"lon": peer},
            device_id_type=pl.DeviceIdType.MESH,
        )

    def own(source, target, chunk, which):
        place = place_of(me, chunk)
        return pltpu.make_async_copy(
            source.at[place, :], target.at[place, :], own_sem.at[which, chunk]
        )

    def start_all(source, target, s_sem, r_sem, chunk, which):
        def one(d, carry):
            across(source, target, s_sem, r_sem, chunk, d).start()
            return carry

        lax.fori_loop(1, n, one, 0)
        own(source, target, chunk, which).start()

    def wait_all(source, target, s_sem, r_sem, chunk, which):
        def one(d, carry):
            across(source, target, s_sem, r_sem, chunk, d).wait_recv()
            return carry

        lax.fori_loop(1, n, one, 0)
        own(source, target, chunk, which).wait()

    def wait_sent(source, target, s_sem, r_sem, chunk):
        def one(d, carry):
            across(source, target, s_sem, r_sem, chunk, d).wait_send()
            return carry

        lax.fori_loop(1, n, one, 0)

    forward = (send, recv, send_sem, recv_sem)
    backward = (back, home, back_sem, home_sem)

    pack(order[0])
    above = jnp.where(part > 0, 1, 0)
    below = jnp.where(part < parts_all - 1, 1, 0)
    pl.semaphore_wait(barrier, n - 1 + above + below)

    for place, chunk in enumerate(order):
        if place:
            pack(chunk)
        start_all(*forward, chunk, 0)

    @pl.when(part == 0)
    def _():
        first[pl.ds(0, REACH)] = jnp.zeros((REACH,) + first.shape[1:], jnp.float32)

    @pl.when(part == parts_all - 1)
    def _():
        first[pl.ds(REACH + rows, REACH)] = jnp.zeros((REACH,) + first.shape[1:], jnp.float32)

    up = pltpu.make_async_remote_copy(
        src_ref=first.at[pl.ds(REACH, REACH)],
        dst_ref=first.at[pl.ds(REACH + rows, REACH)],
        send_sem=halo_send.at[0], recv_sem=halo_recv.at[0],
        device_id=beside(-1),
        device_id_type=pl.DeviceIdType.MESH,
    )
    down = pltpu.make_async_remote_copy(
        src_ref=first.at[pl.ds(rows, REACH)],
        dst_ref=first.at[pl.ds(0, REACH)],
        send_sem=halo_send.at[1], recv_sem=halo_recv.at[1],
        device_id=beside(1),
        device_id_type=pl.DeviceIdType.MESH,
    )

    base = share * rows

    def lon_params(row):
        return lon_off[base + row, level], [lon_w[k, base + row, level] for k in range(4)]

    for place, chunk in enumerate(order):
        wait_all(*forward, chunk, 0)

        def along(t, carry):
            for u in range(tile_rows):
                row = chunk * piece + t * tile_rows + u
                field = recv[pl.ds(row, n, stride=slot), :]
                first[REACH + row] = circled(field, *lon_params(row), per)
            return carry

        lax.fori_loop(0, piece // tile_rows, along, 0)
        if place == min(1, len(order) - 1):

            @pl.when(part > 0)
            def _():
                up.start()

            @pl.when(part < parts_all - 1)
            def _():
                down.start()

    @pl.when(part > 0)
    def _():
        up.wait_send()
        down.wait_recv()

    @pl.when(part < parts_all - 1)
    def _():
        down.wait_send()
        up.wait_recv()

    first_row = part * rows
    for chunk in range(chunks):

        def both(t, carry):
            for u in range(tile_rows):
                row = chunk * piece + t * tile_rows + u
                shift = lat_off[base + row, level]
                field = None
                for k in range(4):
                    source = jnp.clip(first_row + row - shift + (k - 1), 0, parts_all * rows - 1)
                    term = lat_w[k, base + row, level] * first[source - first_row + REACH]
                    field = term if field is None else field + term
                back[pl.ds(row, n, stride=slot), :] = circled(field, *lon_params(row), per)
            return carry

        lax.fori_loop(0, piece // tile_rows, both, 0)
        start_all(*backward, chunk, 1)

    for chunk in range(chunks):
        wait_all(*backward, chunk, 1)

        for s in range(split):

            def unpack(t, carry):
                row = chunk * piece + t * tile_rows
                start = (s * rows + row) * groups
                parts = [
                    home[pl.ds(pl.multiple_of((g * split + s) * slot + row, tile_rows), tile_rows), :]
                    for g in range(groups)
                ]
                for i, block in enumerate(turned(parts, per)):
                    out_ref[pl.ds(start + i, tile_rows, stride=groups), :] = block
                return carry

            lax.fori_loop(0, piece // tile_rows, unpack, 0)

    for chunk in range(chunks):
        wait_sent(*forward, chunk)
        wait_sent(*backward, chunk)


def per_device(tracers, lon_offset, lon_weights, lat_offset, lat_weights):
    rows, width, columns = tracers.shape
    n, bands = lax.axis_size("lon"), lax.axis_size("band")
    groups = width
    per = columns // groups
    per_level = columns // lon_offset.shape[1]
    assert n % groups == 0 and rows % (n // groups) == 0 and per_level % per == 0
    share = rows // (n // groups)
    piece = PIECE if share % PIECE == 0 else share
    chunks = share // piece
    slot = -(-share // SUB) * SUB
    smem = pl.BlockSpec(memory_space=pltpu.SMEM)
    vmem = pl.BlockSpec(memory_space=pltpu.VMEM)
    flat = pltpu.VMEM((n * slot, columns), jnp.float32)
    sems = pltpu.SemaphoreType.DMA((chunks, n))
    out = pl.pallas_call(
        functools.partial(kernel, n, bands, groups, share, piece, per, per_level),
        out_shape=jax.ShapeDtypeStruct((rows * width, columns), jnp.float32),
        in_specs=[vmem, smem, smem, smem, smem],
        out_specs=vmem,
        scratch_shapes=[
            flat,
            flat,
            pltpu.VMEM((share + 2 * REACH, n, columns), jnp.float32),
            flat,
            flat,
            sems,
            sems,
            sems,
            sems,
            pltpu.SemaphoreType.DMA((2,)),
            pltpu.SemaphoreType.DMA((2,)),
            pltpu.SemaphoreType.DMA((2, chunks)),
        ],
        compiler_params=pltpu.CompilerParams(collective_id=0, has_side_effects=True),
    )(tracers.reshape(rows * width, columns), lon_offset, lon_weights, lat_offset, lat_weights)
    return out.reshape(rows, width, columns)


def solution(mesh):
    return jax.shard_map(
        per_device,
        mesh=mesh,
        in_specs=(
            P("band", "lon", None),
            P("band", None),
            P(None, "band", None),
            P("band", None),
            P(None, "band", None),
        ),
        out_specs=P("band", "lon", None),
        check_vma=False,
    )
```

```python
import functools
import math

import jax
import jax.numpy as jnp
from jax import lax
from jax.experimental import pallas as pl
from jax.experimental.pallas import tpu as pltpu
from jax.sharding import PartitionSpec as P

TMAX = 6
REACH = TMAX + 2
SUB = 8
PIECE = 16


def turned(parts, per):
    parts = list(parts)
    count = len(parts)
    lanes = parts[0].shape[1]
    block = lax.broadcasted_iota(jnp.int32, parts[0].shape, 1) // per
    bit = count // 2
    while bit:
        high = (block // bit) % 2 == 1
        move = per * bit
        for i in range(count):
            if i & bit:
                continue
            a, b = parts[i], parts[i | bit]
            parts[i] = jnp.where(high, pltpu.roll(b, move, 1), a)
            parts[i | bit] = jnp.where(high, b, pltpu.roll(a, lanes - move, 1))
        bit //= 2
    return parts


def circled(field, offset, weights, per):
    count, lanes = field.shape
    lane = lax.broadcasted_iota(jnp.int32, field.shape, 1)
    following = pltpu.roll(field, count - 1, 0)
    total = weights[0] * field
    for k in range(1, 4):
        mixed = jnp.where(lane >= per * k, field, following)
        total = total + weights[k] * pltpu.roll(mixed, lanes - per * k, 1)
    shift = ((offset + 1) * per + count * lanes) % (count * lanes)
    coarse, fine = shift // lanes, shift % lanes
    near = pltpu.roll(total, coarse, 0)
    far = pltpu.roll(near, 1, 0)
    return pltpu.roll(jnp.where(lane < lanes - fine, near, far), fine, 1)


def kernel(
    n, bands, groups, rows, piece, per, per_level,
    x_hbm, lon_off_hbm, lon_w_hbm, lat_off_hbm, lat_w_hbm, out_hbm,
    x_ref, lon_off, lon_w, lat_off, lat_w, out_ref,
    send, recv, first, back, home, halo,
    in_sem, out_sem, param_sem, send_sem, recv_sem, back_sem, home_sem, halo_send, halo_recv,
):
    me = lax.axis_index("lon")
    band = lax.axis_index("band")
    split = n // groups
    group, share = me // split, me % split
    part = band * split + share
    parts_all = bands * split
    level = group * per // per_level
    chunks = rows // piece
    tile_rows = math.gcd(SUB, piece)
    slot = send.shape[0] // n
    block = piece * groups
    forwards = band % 2 == 1
    base = share * rows

    def chunk_at(step):
        return jnp.where(forwards, step, chunks - 1 - step)

    def fetch(step, s):
        place = pl.ds(pl.multiple_of((s * rows + chunk_at(step) * piece) * groups, SUB), block)
        return pltpu.make_async_copy(x_hbm.at[place, :], x_ref.at[place, :], in_sem.at[step, s])

    def deliver(step, s):
        place = pl.ds(pl.multiple_of((s * rows + chunk_at(step) * piece) * groups, SUB), block)
        return pltpu.make_async_copy(out_ref.at[place, :], out_hbm.at[place, :], out_sem.at[step, s])

    for step in range(chunks):
        for s in range(split):
            fetch(step, s).start()
    params = [
        pltpu.make_async_copy(source, target, param_sem.at[i])
        for i, (source, target) in enumerate(
            ((lon_off_hbm, lon_off), (lon_w_hbm, lon_w), (lat_off_hbm, lat_off), (lat_w_hbm, lat_w))
        )
    ]
    for param in params:
        param.start()

    barrier = pltpu.get_barrier_semaphore()

    def greet(d, carry):
        pl.semaphore_signal(
            barrier, inc=1, device_id={"lon": lax.rem(me + d, n)},
            device_id_type=pl.DeviceIdType.MESH,
        )
        return carry

    lax.fori_loop(1, n, greet, 0)

    def beside(step):
        other = lax.rem(part + step + parts_all, parts_all)
        return {"band": other // split, "lon": group * split + other % split}

    @pl.when(part > 0)
    def _():
        pl.semaphore_signal(
            barrier, inc=1, device_id=beside(-1), device_id_type=pl.DeviceIdType.MESH
        )

    @pl.when(part < parts_all - 1)
    def _():
        pl.semaphore_signal(
            barrier, inc=1, device_id=beside(1), device_id_type=pl.DeviceIdType.MESH
        )

    def pack(step):
        for s in range(split):
            fetch(step, s).wait()

            def tile(t, carry):
                row = chunk_at(step) * piece + t * tile_rows
                start = (s * rows + row) * groups
                parts = [
                    x_ref[pl.ds(start + i, tile_rows, stride=groups), :] for i in range(groups)
                ]
                for g, part_block in enumerate(turned(parts, per)):
                    to = (g * split + s) * slot + row
                    send[pl.ds(pl.multiple_of(to, tile_rows), tile_rows), :] = part_block
                return carry

            lax.fori_loop(0, piece // tile_rows, tile, 0)

    def place_of(peer, step):
        return pl.ds(pl.multiple_of(peer * slot + chunk_at(step) * piece, SUB), piece)

    def start_all(source, target, s_sem, r_sem, step):
        def one(d, carry):
            peer = lax.rem(me + d, n)
            pltpu.make_async_remote_copy(
                src_ref=source.at[place_of(peer, step), :],
                dst_ref=target.at[place_of(me, step), :],
                send_sem=s_sem,
                recv_sem=r_sem.at[step],
                device_id={"lon": peer},
                device_id_type=pl.DeviceIdType.MESH,
            ).start()
            return carry

        place = place_of(me, step)
        pltpu.make_async_copy(source.at[place, :], target.at[place, :], r_sem.at[step]).start()
        lax.fori_loop(1, n, one, 0)

    def wait_bytes(ref, sem, count):
        whole = ref.at[pl.ds(0, count), :]
        pltpu.make_async_copy(whole, whole, sem).wait()

    forward = (send, recv, send_sem, recv_sem)
    backward = (back, home, back_sem, home_sem)

    pack(0)
    above = jnp.where(part > 0, 1, 0)
    below = jnp.where(part < parts_all - 1, 1, 0)
    pl.semaphore_wait(barrier, n - 1 + above + below)
    start_all(*forward, 0)
    for step in range(1, chunks):
        pack(step)
        start_all(*forward, step)

    for param in params:
        param.wait()

    up = pltpu.make_async_remote_copy(
        src_ref=first.at[pl.ds(REACH, REACH)],
        dst_ref=halo.at[1],
        send_sem=halo_send.at[0], recv_sem=halo_recv.at[1],
        device_id=beside(-1),
        device_id_type=pl.DeviceIdType.MESH,
    )
    down = pltpu.make_async_remote_copy(
        src_ref=first.at[pl.ds(rows, REACH)],
        dst_ref=halo.at[0],
        send_sem=halo_send.at[1], recv_sem=halo_recv.at[0],
        device_id=beside(1),
        device_id_type=pl.DeviceIdType.MESH,
    )
    has_up, has_down = part > 0, part < parts_all - 1

    def send_edges(low, high):
        @pl.when(jnp.logical_and(low, has_up))
        def _():
            up.start()

        @pl.when(jnp.logical_and(high, has_down))
        def _():
            down.start()

    def take_edges(low, high):
        @pl.when(jnp.logical_and(low, has_up))
        def _():
            down.wait_recv()
            first[pl.ds(0, REACH)] = halo[0]

        @pl.when(jnp.logical_and(high, has_down))
        def _():
            up.wait_recv()
            first[pl.ds(REACH + rows, REACH)] = halo[1]

    backwards = jnp.logical_not(forwards)

    def lon_params(row):
        return lon_off[level, base + row], [lon_w[k, level, base + row] for k in range(4)]

    def along(step):
        def some(t, carry):
            for u in range(tile_rows):
                row = chunk_at(step) * piece + t * tile_rows + u
                field = recv[pl.ds(row, n, stride=slot), :]
                first[REACH + row] = circled(field, *lon_params(row), per)
            return carry

        lax.fori_loop(0, piece // tile_rows, some, 0)

    first_row = part * rows

    def across_and_along(step):
        def some(t, carry):
            for u in range(tile_rows):
                row = chunk_at(step) * piece + t * tile_rows + u
                shift = lat_off[level, base + row]
                field = None
                for k in range(4):
                    source = jnp.clip(first_row + row - shift + (k - 1), 0, parts_all * rows - 1)
                    term = lat_w[k, level, base + row] * first[source - first_row + REACH]
                    field = term if field is None else field + term
                back[pl.ds(row, n, stride=slot), :] = circled(field, *lon_params(row), per)
            return carry

        lax.fori_loop(0, piece // tile_rows, some, 0)

    for step in range(chunks):
        wait_bytes(recv, recv_sem.at[step], n * piece)
        along(step)
        if chunks == 1:
            send_edges(True, True)
        elif step == 0:
            send_edges(forwards, backwards)
        elif step == chunks - 1:
            send_edges(backwards, forwards)
        if step:
            if step == 1:
                take_edges(forwards, backwards)
            across_and_along(step - 1)
            start_all(*backward, step - 1)
    if chunks == 1:
        take_edges(True, True)
    else:
        take_edges(backwards, forwards)
    across_and_along(chunks - 1)
    start_all(*backward, chunks - 1)

    for step in range(chunks):
        wait_bytes(home, home_sem.at[step], n * piece)
        for s in range(split):

            def unpack(t, carry):
                row = chunk_at(step) * piece + t * tile_rows
                start = (s * rows + row) * groups
                parts = [
                    home[pl.ds(pl.multiple_of((g * split + s) * slot + row, tile_rows), tile_rows), :]
                    for g in range(groups)
                ]
                for i, part_block in enumerate(turned(parts, per)):
                    out_ref[pl.ds(start + i, tile_rows, stride=groups), :] = part_block
                return carry

            lax.fori_loop(0, piece // tile_rows, unpack, 0)
            deliver(step, s).start()

    wait_bytes(send, send_sem, (n - 1) * rows)
    wait_bytes(back, back_sem, (n - 1) * rows)

    @pl.when(has_up)
    def _():
        up.wait_send()

    @pl.when(has_down)
    def _():
        down.wait_send()

    for step in range(chunks):
        for s in range(split):
            deliver(step, s).wait()


def per_device(tracers, lon_offset, lon_weights, lat_offset, lat_weights):
    rows, width, columns = tracers.shape
    n, bands = lax.axis_size("lon"), lax.axis_size("band")
    groups = width
    per = columns // groups
    levels = lon_offset.shape[1]
    per_level = columns // levels
    split = n // groups
    assert n % groups == 0 and rows % split == 0 and per_level % per == 0
    share = rows // split
    piece = PIECE if share % PIECE == 0 else share
    chunks = share // piece
    slot = -(-share // SUB) * SUB
    flat = pltpu.VMEM((n * slot, columns), jnp.float32)
    whole = pltpu.VMEM((rows * width, columns), jnp.float32)
    dma = pltpu.SemaphoreType.DMA
    out = pl.pallas_call(
        functools.partial(kernel, n, bands, groups, share, piece, per, per_level),
        out_shape=jax.ShapeDtypeStruct((rows * width, columns), jnp.float32),
        in_specs=[pl.BlockSpec(memory_space=pl.ANY)] * 5,
        out_specs=pl.BlockSpec(memory_space=pl.ANY),
        scratch_shapes=[
            whole,
            pltpu.SMEM((levels, rows), jnp.int32),
            pltpu.SMEM((4, levels, rows), jnp.float32),
            pltpu.SMEM((levels, rows), jnp.int32),
            pltpu.SMEM((4, levels, rows), jnp.float32),
            whole,
            flat,
            flat,
            pltpu.VMEM((share + 2 * REACH, n, columns), jnp.float32),
            flat,
            flat,
            pltpu.VMEM((2, REACH, n, columns), jnp.float32),
            dma((chunks, split)),
            dma((chunks, split)),
            dma((4,)),
            dma,
            dma((chunks,)),
            dma,
            dma((chunks,)),
            dma((2,)),
            dma((2,)),
        ],
        compiler_params=pltpu.CompilerParams(collective_id=0, has_side_effects=True),
    )(
        tracers.reshape(rows * width, columns),
        lon_offset.T,
        lon_weights.transpose(0, 2, 1),
        lat_offset.T,
        lat_weights.transpose(0, 2, 1),
    )
    return out.reshape(rows, width, columns)


def solution(mesh):
    return jax.shard_map(
        per_device,
        mesh=mesh,
        in_specs=(
            P("band", "lon", None),
            P("band", None),
            P(None, "band", None),
            P("band", None),
            P(None, "band", None),
        ),
        out_specs=P("band", "lon", None),
        check_vma=False,
    )
```

```python
import functools
import math

import jax
import jax.numpy as jnp
from jax import lax
from jax.experimental import pallas as pl
from jax.experimental.pallas import tpu as pltpu
from jax.sharding import PartitionSpec as P

TMAX = 6
REACH = TMAX + 2
SUB = 8
PIECE = 16


def turned(parts, per):
    parts = list(parts)
    count = len(parts)
    lanes = parts[0].shape[1]
    block = lax.broadcasted_iota(jnp.int32, parts[0].shape, 1) // per
    bit = count // 2
    while bit:
        high = (block // bit) % 2 == 1
        move = per * bit
        for i in range(count):
            if i & bit:
                continue
            a, b = parts[i], parts[i | bit]
            parts[i] = jnp.where(high, pltpu.roll(b, move, 1), a)
            parts[i | bit] = jnp.where(high, b, pltpu.roll(a, lanes - move, 1))
        bit //= 2
    return parts


def circled(field, offset, weights, per):
    count, lanes = field.shape
    lane = lax.broadcasted_iota(jnp.int32, field.shape, 1)
    following = pltpu.roll(field, count - 1, 0)
    total = weights[0] * field
    for k in range(1, 4):
        mixed = jnp.where(lane >= per * k, field, following)
        total = total + weights[k] * pltpu.roll(mixed, lanes - per * k, 1)
    shift = ((offset + 1) * per + count * lanes) % (count * lanes)
    coarse, fine = shift // lanes, shift % lanes
    near = pltpu.roll(total, coarse, 0)
    far = pltpu.roll(near, 1, 0)
    return pltpu.roll(jnp.where(lane < lanes - fine, near, far), fine, 1)


def kernel(
    n, bands, groups, rows, piece, per, per_level,
    x_hbm, lon_off_hbm, lon_w_hbm, lat_off_hbm, lat_w_hbm, out_ref,
    x_ref, lon_off, lon_w, lat_off, lat_w,
    send, recv, first, back, home, halo,
    in_sem, param_sem, send_sem, recv_sem, back_sem, home_sem, halo_send, halo_recv,
):
    me = lax.axis_index("lon")
    band = lax.axis_index("band")
    split = n // groups
    group, share = me // split, me % split
    part = band * split + share
    parts_all = bands * split
    level = group * per // per_level
    chunks = rows // piece
    tile_rows = math.gcd(SUB, piece)
    slot = send.shape[0] // n
    block = piece * groups
    forwards = band % 2 == 1
    base = share * rows

    def chunk_at(step):
        return jnp.where(forwards, step, chunks - 1 - step)

    def fetch(step, s):
        place = pl.ds(pl.multiple_of((s * rows + chunk_at(step) * piece) * groups, SUB), block)
        return pltpu.make_async_copy(x_hbm.at[place, :], x_ref.at[place, :], in_sem.at[step, s])

    for step in range(chunks):
        for s in range(split):
            fetch(step, s).start()
    params = [
        pltpu.make_async_copy(source, target, param_sem.at[i])
        for i, (source, target) in enumerate(
            ((lon_off_hbm, lon_off), (lon_w_hbm, lon_w), (lat_off_hbm, lat_off), (lat_w_hbm, lat_w))
        )
    ]
    for param in params:
        param.start()

    barrier = pltpu.get_barrier_semaphore()

    def greet(d, carry):
        pl.semaphore_signal(
            barrier, inc=1, device_id={"lon": lax.rem(me + d, n)},
            device_id_type=pl.DeviceIdType.MESH,
        )
        return carry

    lax.fori_loop(1, n, greet, 0)

    def beside(step):
        other = lax.rem(part + step + parts_all, parts_all)
        return {"band": other // split, "lon": group * split + other % split}

    @pl.when(part > 0)
    def _():
        pl.semaphore_signal(
            barrier, inc=1, device_id=beside(-1), device_id_type=pl.DeviceIdType.MESH
        )

    @pl.when(part < parts_all - 1)
    def _():
        pl.semaphore_signal(
            barrier, inc=1, device_id=beside(1), device_id_type=pl.DeviceIdType.MESH
        )

    def pack(step):
        for s in range(split):
            fetch(step, s).wait()

            def tile(t, carry):
                row = chunk_at(step) * piece + t * tile_rows
                start = (s * rows + row) * groups
                parts = [
                    x_ref[pl.ds(start + i, tile_rows, stride=groups), :] for i in range(groups)
                ]
                for g, part_block in enumerate(turned(parts, per)):
                    to = (g * split + s) * slot + row
                    send[pl.ds(pl.multiple_of(to, tile_rows), tile_rows), :] = part_block
                return carry

            lax.fori_loop(0, piece // tile_rows, tile, 0)

    def place_of(peer, step):
        return pl.ds(pl.multiple_of(peer * slot + chunk_at(step) * piece, SUB), piece)

    def start_all(source, target, s_sem, r_sem, step):
        def one(i, carry):
            peer = lax.rem(me + i // 2 + jnp.where(i % 2 == 0, n // 2, 1), n)
            pltpu.make_async_remote_copy(
                src_ref=source.at[place_of(peer, step), :],
                dst_ref=target.at[place_of(me, step), :],
                send_sem=s_sem,
                recv_sem=r_sem.at[step],
                device_id={"lon": peer},
                device_id_type=pl.DeviceIdType.MESH,
            ).start()
            return carry

        place = place_of(me, step)
        pltpu.make_async_copy(source.at[place, :], target.at[place, :], r_sem.at[step]).start()
        lax.fori_loop(0, n - 1, one, 0)

    def wait_bytes(ref, sem, count):
        whole = ref.at[pl.ds(0, count), :]
        pltpu.make_async_copy(whole, whole, sem).wait()

    forward = (send, recv, send_sem, recv_sem)
    backward = (back, home, back_sem, home_sem)

    pack(0)
    above = jnp.where(part > 0, 1, 0)
    below = jnp.where(part < parts_all - 1, 1, 0)
    pl.semaphore_wait(barrier, n - 1 + above + below)
    start_all(*forward, 0)
    for step in range(1, chunks):
        pack(step)
        start_all(*forward, step)

    for param in params:
        param.wait()

    up = pltpu.make_async_remote_copy(
        src_ref=first.at[pl.ds(REACH, REACH)],
        dst_ref=halo.at[1],
        send_sem=halo_send.at[0], recv_sem=halo_recv.at[1],
        device_id=beside(-1),
        device_id_type=pl.DeviceIdType.MESH,
    )
    down = pltpu.make_async_remote_copy(
        src_ref=first.at[pl.ds(rows, REACH)],
        dst_ref=halo.at[0],
        send_sem=halo_send.at[1], recv_sem=halo_recv.at[0],
        device_id=beside(1),
        device_id_type=pl.DeviceIdType.MESH,
    )
    has_up, has_down = part > 0, part < parts_all - 1

    def send_edges(low, high):
        @pl.when(jnp.logical_and(low, has_up))
        def _():
            up.start()

        @pl.when(jnp.logical_and(high, has_down))
        def _():
            down.start()

    def take_edges(low, high):
        @pl.when(jnp.logical_and(low, has_up))
        def _():
            down.wait_recv()
            first[pl.ds(0, REACH)] = halo[0]

        @pl.when(jnp.logical_and(high, has_down))
        def _():
            up.wait_recv()
            first[pl.ds(REACH + rows, REACH)] = halo[1]

    backwards = jnp.logical_not(forwards)

    def lon_params(row):
        return lon_off[level, base + row], [lon_w[k, level, base + row] for k in range(4)]

    def along(step):
        def some(t, carry):
            for u in range(tile_rows):
                row = chunk_at(step) * piece + t * tile_rows + u
                field = recv[pl.ds(row, n, stride=slot), :]
                first[REACH + row] = circled(field, *lon_params(row), per)
            return carry

        lax.fori_loop(0, piece // tile_rows, some, 0)

    first_row = part * rows

    def across_and_along(step):
        def some(t, carry):
            for u in range(tile_rows):
                row = chunk_at(step) * piece + t * tile_rows + u
                shift = lat_off[level, base + row]
                field = None
                for k in range(4):
                    source = jnp.clip(first_row + row - shift + (k - 1), 0, parts_all * rows - 1)
                    term = lat_w[k, level, base + row] * first[source - first_row + REACH]
                    field = term if field is None else field + term
                back[pl.ds(row, n, stride=slot), :] = circled(field, *lon_params(row), per)
            return carry

        lax.fori_loop(0, piece // tile_rows, some, 0)

    for step in range(chunks):
        wait_bytes(recv, recv_sem.at[step], n * piece)
        along(step)
        if chunks == 1:
            send_edges(True, True)
        elif step == 0:
            send_edges(forwards, backwards)
        elif step == chunks - 1:
            send_edges(backwards, forwards)
        if step:
            if step == 1:
                take_edges(forwards, backwards)
            across_and_along(step - 1)
            start_all(*backward, step - 1)
    if chunks == 1:
        take_edges(True, True)
    else:
        take_edges(backwards, forwards)
    across_and_along(chunks - 1)
    start_all(*backward, chunks - 1)

    for step in range(chunks):
        wait_bytes(home, home_sem.at[step], n * piece)
        for s in range(split):

            def unpack(t, carry):
                row = chunk_at(step) * piece + t * tile_rows
                start = (s * rows + row) * groups
                parts = [
                    home[pl.ds(pl.multiple_of((g * split + s) * slot + row, tile_rows), tile_rows), :]
                    for g in range(groups)
                ]
                for i, part_block in enumerate(turned(parts, per)):
                    out_ref[pl.ds(start + i, tile_rows, stride=groups), :] = part_block
                return carry

            lax.fori_loop(0, piece // tile_rows, unpack, 0)

    wait_bytes(send, send_sem, (n - 1) * rows)
    wait_bytes(back, back_sem, (n - 1) * rows)

    @pl.when(has_up)
    def _():
        up.wait_send()

    @pl.when(has_down)
    def _():
        down.wait_send()


def per_device(tracers, lon_offset, lon_weights, lat_offset, lat_weights):
    rows, width, columns = tracers.shape
    n, bands = lax.axis_size("lon"), lax.axis_size("band")
    groups = width
    per = columns // groups
    levels = lon_offset.shape[1]
    per_level = columns // levels
    split = n // groups
    assert n % groups == 0 and rows % split == 0 and per_level % per == 0
    share = rows // split
    piece = PIECE if share % PIECE == 0 else share
    chunks = share // piece
    slot = -(-share // SUB) * SUB
    flat = pltpu.VMEM((n * slot, columns), jnp.float32)
    whole = pltpu.VMEM((rows * width, columns), jnp.float32)
    dma = pltpu.SemaphoreType.DMA
    out = pl.pallas_call(
        functools.partial(kernel, n, bands, groups, share, piece, per, per_level),
        out_shape=whole,
        in_specs=[pl.BlockSpec(memory_space=pl.ANY)] * 5,
        out_specs=pl.BlockSpec(memory_space=pltpu.VMEM),
        scratch_shapes=[
            whole,
            pltpu.SMEM((levels, rows), jnp.int32),
            pltpu.SMEM((4, levels, rows), jnp.float32),
            pltpu.SMEM((levels, rows), jnp.int32),
            pltpu.SMEM((4, levels, rows), jnp.float32),
            flat,
            flat,
            pltpu.VMEM((share + 2 * REACH, n, columns), jnp.float32),
            flat,
            flat,
            pltpu.VMEM((2, REACH, n, columns), jnp.float32),
            dma((chunks, split)),
            dma((4,)),
            dma,
            dma((chunks,)),
            dma,
            dma((chunks,)),
            dma((2,)),
            dma((2,)),
        ],
        compiler_params=pltpu.CompilerParams(collective_id=0, has_side_effects=True),
    )(
        tracers.reshape(rows * width, columns),
        lon_offset.T,
        lon_weights.transpose(0, 2, 1),
        lat_offset.T,
        lat_weights.transpose(0, 2, 1),
    )
    return out.reshape(rows, width, columns)


def solution(mesh):
    return jax.shard_map(
        per_device,
        mesh=mesh,
        in_specs=(
            P("band", "lon", None),
            P("band", None),
            P(None, "band", None),
            P("band", None),
            P(None, "band", None),
        ),
        out_specs=P("band", "lon", None),
        check_vma=False,
    )
```

```python
import functools
import math

import jax
import jax.numpy as jnp
from jax import lax
from jax.experimental import pallas as pl
from jax.experimental.pallas import tpu as pltpu
from jax.sharding import PartitionSpec as P

TMAX = 6
REACH = TMAX + 2
SUB = 8
PIECE = 8


def turned(parts, per):
    parts = list(parts)
    count = len(parts)
    lanes = parts[0].shape[1]
    block = lax.broadcasted_iota(jnp.int32, parts[0].shape, 1) // per
    bit = count // 2
    while bit:
        high = (block // bit) % 2 == 1
        move = per * bit
        for i in range(count):
            if i & bit:
                continue
            a, b = parts[i], parts[i | bit]
            parts[i] = jnp.where(high, pltpu.roll(b, move, 1), a)
            parts[i | bit] = jnp.where(high, b, pltpu.roll(a, lanes - move, 1))
        bit //= 2
    return parts


def circled(field, offset, weights, per):
    count, lanes = field.shape
    lane = lax.broadcasted_iota(jnp.int32, field.shape, 1)
    following = pltpu.roll(field, count - 1, 0)
    total = weights[0] * field
    for k in range(1, 4):
        mixed = jnp.where(lane >= per * k, field, following)
        total = total + weights[k] * pltpu.roll(mixed, lanes - per * k, 1)
    shift = ((offset + 1) * per + count * lanes) % (count * lanes)
    coarse, fine = shift // lanes, shift % lanes
    near = pltpu.roll(total, coarse, 0)
    far = pltpu.roll(near, 1, 0)
    return pltpu.roll(jnp.where(lane < lanes - fine, near, far), fine, 1)


def kernel(
    n, bands, groups, rows, piece, per, per_level,
    x_hbm, lon_off_hbm, lon_w_hbm, lat_off_hbm, lat_w_hbm, out_ref,
    x_ref, lon_off, lon_w, lat_off, lat_w,
    send, recv, first, back, home, halo,
    in_sem, param_sem, send_sem, recv_sem, back_sem, home_sem, halo_send, halo_recv,
):
    me = lax.axis_index("lon")
    band = lax.axis_index("band")
    split = n // groups
    group, share = me // split, me % split
    part = band * split + share
    parts_all = bands * split
    level = group * per // per_level
    chunks = rows // piece
    tile_rows = math.gcd(SUB, piece)
    slot = send.shape[0] // n
    block = piece * groups
    forwards = band % 2 == 1
    base = share * rows

    def chunk_at(step):
        return jnp.where(forwards, step, chunks - 1 - step)

    def fetch(step, s):
        place = pl.ds(pl.multiple_of((s * rows + chunk_at(step) * piece) * groups, SUB), block)
        return pltpu.make_async_copy(x_hbm.at[place, :], x_ref.at[place, :], in_sem.at[step, s])

    for step in range(chunks):
        for s in range(split):
            fetch(step, s).start()
    params = [
        pltpu.make_async_copy(source, target, param_sem.at[i])
        for i, (source, target) in enumerate(
            ((lon_off_hbm, lon_off), (lon_w_hbm, lon_w), (lat_off_hbm, lat_off), (lat_w_hbm, lat_w))
        )
    ]
    for param in params:
        param.start()

    barrier = pltpu.get_barrier_semaphore()

    def greet(d, carry):
        pl.semaphore_signal(
            barrier, inc=1, device_id={"lon": lax.rem(me + d, n)},
            device_id_type=pl.DeviceIdType.MESH,
        )
        return carry

    lax.fori_loop(1, n, greet, 0)

    def beside(step):
        other = lax.rem(part + step + parts_all, parts_all)
        return {"band": other // split, "lon": group * split + other % split}

    @pl.when(part > 0)
    def _():
        pl.semaphore_signal(
            barrier, inc=1, device_id=beside(-1), device_id_type=pl.DeviceIdType.MESH
        )

    @pl.when(part < parts_all - 1)
    def _():
        pl.semaphore_signal(
            barrier, inc=1, device_id=beside(1), device_id_type=pl.DeviceIdType.MESH
        )

    def pack(step):
        for s in range(split):
            fetch(step, s).wait()

            def tile(t, carry):
                row = chunk_at(step) * piece + t * tile_rows
                start = (s * rows + row) * groups
                parts = [
                    x_ref[pl.ds(start + i, tile_rows, stride=groups), :] for i in range(groups)
                ]
                for g, part_block in enumerate(turned(parts, per)):
                    to = (g * split + s) * slot + row
                    send[pl.ds(pl.multiple_of(to, tile_rows), tile_rows), :] = part_block
                return carry

            lax.fori_loop(0, piece // tile_rows, tile, 0)

    def place_of(peer, step):
        return pl.ds(pl.multiple_of(peer * slot + chunk_at(step) * piece, SUB), piece)

    def start_all(source, target, s_sem, r_sem, step):
        def one(i, carry):
            peer = lax.rem(me + i // 2 + jnp.where(i % 2 == 0, n // 2, 1), n)
            pltpu.make_async_remote_copy(
                src_ref=source.at[place_of(peer, step), :],
                dst_ref=target.at[place_of(me, step), :],
                send_sem=s_sem,
                recv_sem=r_sem.at[step],
                device_id={"lon": peer},
                device_id_type=pl.DeviceIdType.MESH,
            ).start()
            return carry

        place = place_of(me, step)
        pltpu.make_async_copy(source.at[place, :], target.at[place, :], r_sem.at[step]).start()
        lax.fori_loop(0, n - 1, one, 0)

    def wait_bytes(ref, sem, count):
        whole = ref.at[pl.ds(0, count), :]
        pltpu.make_async_copy(whole, whole, sem).wait()

    forward = (send, recv, send_sem, recv_sem)
    backward = (back, home, back_sem, home_sem)

    pack(0)
    above = jnp.where(part > 0, 1, 0)
    below = jnp.where(part < parts_all - 1, 1, 0)
    pl.semaphore_wait(barrier, n - 1 + above + below)
    start_all(*forward, 0)
    for step in range(1, chunks):
        pack(step)
        start_all(*forward, step)

    for param in params:
        param.wait()

    up = pltpu.make_async_remote_copy(
        src_ref=first.at[pl.ds(REACH, REACH)],
        dst_ref=halo.at[1],
        send_sem=halo_send.at[0], recv_sem=halo_recv.at[1],
        device_id=beside(-1),
        device_id_type=pl.DeviceIdType.MESH,
    )
    down = pltpu.make_async_remote_copy(
        src_ref=first.at[pl.ds(rows, REACH)],
        dst_ref=halo.at[0],
        send_sem=halo_send.at[1], recv_sem=halo_recv.at[0],
        device_id=beside(1),
        device_id_type=pl.DeviceIdType.MESH,
    )
    has_up, has_down = part > 0, part < parts_all - 1

    def send_edges(low, high):
        @pl.when(jnp.logical_and(low, has_up))
        def _():
            up.start()

        @pl.when(jnp.logical_and(high, has_down))
        def _():
            down.start()

    def take_edges(low, high):
        @pl.when(jnp.logical_and(low, has_up))
        def _():
            down.wait_recv()
            first[pl.ds(0, REACH)] = halo[0]

        @pl.when(jnp.logical_and(high, has_down))
        def _():
            up.wait_recv()
            first[pl.ds(REACH + rows, REACH)] = halo[1]

    backwards = jnp.logical_not(forwards)

    def lon_params(row):
        return lon_off[level, base + row], [lon_w[k, level, base + row] for k in range(4)]

    def along(step):
        def some(t, carry):
            for u in range(tile_rows):
                row = chunk_at(step) * piece + t * tile_rows + u
                field = recv[pl.ds(row, n, stride=slot), :]
                first[REACH + row] = circled(field, *lon_params(row), per)
            return carry

        lax.fori_loop(0, piece // tile_rows, some, 0)

    first_row = part * rows

    def across_and_along(step):
        def some(t, carry):
            for u in range(tile_rows):
                row = chunk_at(step) * piece + t * tile_rows + u
                shift = lat_off[level, base + row]
                field = None
                for k in range(4):
                    source = jnp.clip(first_row + row - shift + (k - 1), 0, parts_all * rows - 1)
                    term = lat_w[k, level, base + row] * first[source - first_row + REACH]
                    field = term if field is None else field + term
                back[pl.ds(row, n, stride=slot), :] = circled(field, *lon_params(row), per)
            return carry

        lax.fori_loop(0, piece // tile_rows, some, 0)

    for step in range(chunks):
        wait_bytes(recv, recv_sem.at[step], n * piece)
        along(step)
        if chunks == 1:
            send_edges(True, True)
        elif step == 0:
            send_edges(forwards, backwards)
        elif step == chunks - 1:
            send_edges(backwards, forwards)
        if step:
            if step == 1:
                take_edges(forwards, backwards)
            across_and_along(step - 1)
            start_all(*backward, step - 1)
    if chunks == 1:
        take_edges(True, True)
    else:
        take_edges(backwards, forwards)
    across_and_along(chunks - 1)
    start_all(*backward, chunks - 1)

    for step in range(chunks):
        wait_bytes(home, home_sem.at[step], n * piece)
        for s in range(split):

            def unpack(t, carry):
                row = chunk_at(step) * piece + t * tile_rows
                start = (s * rows + row) * groups
                parts = [
                    home[pl.ds(pl.multiple_of((g * split + s) * slot + row, tile_rows), tile_rows), :]
                    for g in range(groups)
                ]
                for i, part_block in enumerate(turned(parts, per)):
                    out_ref[pl.ds(start + i, tile_rows, stride=groups), :] = part_block
                return carry

            lax.fori_loop(0, piece // tile_rows, unpack, 0)

    wait_bytes(send, send_sem, (n - 1) * rows)
    wait_bytes(back, back_sem, (n - 1) * rows)

    @pl.when(has_up)
    def _():
        up.wait_send()

    @pl.when(has_down)
    def _():
        down.wait_send()


def per_device(tracers, lon_offset, lon_weights, lat_offset, lat_weights):
    rows, width, columns = tracers.shape
    n, bands = lax.axis_size("lon"), lax.axis_size("band")
    groups = width
    per = columns // groups
    levels = lon_offset.shape[1]
    per_level = columns // levels
    split = n // groups
    assert n % groups == 0 and rows % split == 0 and per_level % per == 0
    share = rows // split
    piece = PIECE if share % PIECE == 0 else share
    chunks = share // piece
    slot = -(-share // SUB) * SUB
    flat = pltpu.VMEM((n * slot, columns), jnp.float32)
    whole = pltpu.VMEM((rows * width, columns), jnp.float32)
    dma = pltpu.SemaphoreType.DMA
    out = pl.pallas_call(
        functools.partial(kernel, n, bands, groups, share, piece, per, per_level),
        out_shape=whole,
        in_specs=[pl.BlockSpec(memory_space=pl.ANY)] * 5,
        out_specs=pl.BlockSpec(memory_space=pltpu.VMEM),
        scratch_shapes=[
            whole,
            pltpu.SMEM((levels, rows), jnp.int32),
            pltpu.SMEM((4, levels, rows), jnp.float32),
            pltpu.SMEM((levels, rows), jnp.int32),
            pltpu.SMEM((4, levels, rows), jnp.float32),
            flat,
            flat,
            pltpu.VMEM((share + 2 * REACH, n, columns), jnp.float32),
            flat,
            flat,
            pltpu.VMEM((2, REACH, n, columns), jnp.float32),
            dma((chunks, split)),
            dma((4,)),
            dma,
            dma((chunks,)),
            dma,
            dma((chunks,)),
            dma((2,)),
            dma((2,)),
        ],
        compiler_params=pltpu.CompilerParams(collective_id=0, has_side_effects=True),
    )(
        tracers.reshape(rows * width, columns),
        lon_offset.T,
        lon_weights.transpose(0, 2, 1),
        lat_offset.T,
        lat_weights.transpose(0, 2, 1),
    )
    return out.reshape(rows, width, columns)


def solution(mesh):
    return jax.shard_map(
        per_device,
        mesh=mesh,
        in_specs=(
            P("band", "lon", None),
            P("band", None),
            P(None, "band", None),
            P("band", None),
            P(None, "band", None),
        ),
        out_specs=P("band", "lon", None),
        check_vma=False,
    )
```

```python
import functools
import math

import jax
import jax.numpy as jnp
from jax import lax
from jax.experimental import pallas as pl
from jax.experimental.pallas import tpu as pltpu
from jax.sharding import PartitionSpec as P

TMAX = 6
REACH = TMAX + 2
SUB = 8
PIECE = 8


def turned(parts, per):
    parts = list(parts)
    count = len(parts)
    lanes = parts[0].shape[1]
    block = lax.broadcasted_iota(jnp.int32, parts[0].shape, 1) // per
    bit = count // 2
    while bit:
        high = (block // bit) % 2 == 1
        move = per * bit
        for i in range(count):
            if i & bit:
                continue
            a, b = parts[i], parts[i | bit]
            parts[i] = jnp.where(high, pltpu.roll(b, move, 1), a)
            parts[i | bit] = jnp.where(high, b, pltpu.roll(a, lanes - move, 1))
        bit //= 2
    return parts


def circled(fields, followings, offsets, weights, per, spin):
    count, lanes = fields[0].shape
    lane = lax.broadcasted_iota(jnp.int32, fields[0].shape, 1)
    turns = []
    for u, (field, following) in enumerate(zip(fields, followings)):
        total = weights[u][0] * field
        for k in range(1, 4):
            mixed = jnp.where(lane >= per * k, field, following)
            total = total + weights[u][k] * pltpu.roll(mixed, lanes - per * k, 1)
        shift = ((offsets[u] + 1) * per + count * lanes) % (count * lanes)
        coarse, fine = shift // lanes, shift % lanes
        total = pltpu.roll(total, fine, 1)
        spin[pl.ds(2 * u * count, count), :] = total
        spin[pl.ds((2 * u + 1) * count, count), :] = total
        turns.append((coarse, fine))
    results = []
    for u, (coarse, fine) in enumerate(turns):
        near = spin[pl.ds((2 * u + 1) * count - coarse, count), :]
        far = spin[pl.ds((2 * u + 1) * count - 1 - coarse, count), :]
        results.append(jnp.where(lane >= fine, near, far))
    return results


def kernel(
    n, bands, groups, rows, piece, per, per_level,
    x_hbm, lon_off_hbm, lon_w_hbm, lat_off_hbm, lat_w_hbm, out_ref,
    x_ref, lon_off, lon_w, lat_off, lat_w,
    send, recv, first, back, home, halo, spin,
    in_sem, param_sem, send_sem, recv_sem, back_sem, home_sem, halo_send, halo_recv,
):
    me = lax.axis_index("lon")
    band = lax.axis_index("band")
    split = n // groups
    group, share = me // split, me % split
    part = band * split + share
    parts_all = bands * split
    level = group * per // per_level
    chunks = rows // piece
    tile_rows = math.gcd(SUB, piece)
    slot = send.shape[0] // n
    block = piece * groups
    forwards = band % 2 == 1
    base = share * rows

    def chunk_at(step):
        return jnp.where(forwards, step, chunks - 1 - step)

    def fetch(step, s):
        place = pl.ds(pl.multiple_of((s * rows + chunk_at(step) * piece) * groups, SUB), block)
        return pltpu.make_async_copy(x_hbm.at[place, :], x_ref.at[place, :], in_sem.at[step, s])

    for step in range(chunks):
        for s in range(split):
            fetch(step, s).start()
    params = [
        pltpu.make_async_copy(source, target, param_sem.at[i])
        for i, (source, target) in enumerate(
            ((lon_off_hbm, lon_off), (lon_w_hbm, lon_w), (lat_off_hbm, lat_off), (lat_w_hbm, lat_w))
        )
    ]
    for param in params:
        param.start()

    barrier = pltpu.get_barrier_semaphore()

    def greet(d, carry):
        pl.semaphore_signal(
            barrier, inc=1, device_id={"lon": lax.rem(me + d, n)},
            device_id_type=pl.DeviceIdType.MESH,
        )
        return carry

    lax.fori_loop(1, n, greet, 0)

    def beside(step):
        other = lax.rem(part + step + parts_all, parts_all)
        return {"band": other // split, "lon": group * split + other % split}

    @pl.when(part > 0)
    def _():
        pl.semaphore_signal(
            barrier, inc=1, device_id=beside(-1), device_id_type=pl.DeviceIdType.MESH
        )

    @pl.when(part < parts_all - 1)
    def _():
        pl.semaphore_signal(
            barrier, inc=1, device_id=beside(1), device_id_type=pl.DeviceIdType.MESH
        )

    def pack(step):
        for s in range(split):
            fetch(step, s).wait()

            def tile(t, carry):
                row = chunk_at(step) * piece + t * tile_rows
                start = (s * rows + row) * groups
                parts = [
                    x_ref[pl.ds(start + i, tile_rows, stride=groups), :] for i in range(groups)
                ]
                for g, part_block in enumerate(turned(parts, per)):
                    to = (g * split + s) * slot + row
                    send[pl.ds(pl.multiple_of(to, tile_rows), tile_rows), :] = part_block
                return carry

            lax.fori_loop(0, piece // tile_rows, tile, 0)

    def place_of(peer, step):
        return pl.ds(pl.multiple_of(peer * slot + chunk_at(step) * piece, SUB), piece)

    def start_all(source, target, s_sem, r_sem, step):
        def one(i, carry):
            peer = lax.rem(me + i // 2 + jnp.where(i % 2 == 0, n // 2, 1), n)
            pltpu.make_async_remote_copy(
                src_ref=source.at[place_of(peer, step), :],
                dst_ref=target.at[place_of(me, step), :],
                send_sem=s_sem,
                recv_sem=r_sem.at[step],
                device_id={"lon": peer},
                device_id_type=pl.DeviceIdType.MESH,
            ).start()
            return carry

        place = place_of(me, step)
        pltpu.make_async_copy(source.at[place, :], target.at[place, :], r_sem.at[step]).start()
        lax.fori_loop(0, n - 1, one, 0)

    def wait_bytes(ref, sem, count):
        whole = ref.at[pl.ds(0, count), :]
        pltpu.make_async_copy(whole, whole, sem).wait()

    forward = (send, recv, send_sem, recv_sem)
    backward = (back, home, back_sem, home_sem)

    pack(0)
    above = jnp.where(part > 0, 1, 0)
    below = jnp.where(part < parts_all - 1, 1, 0)
    pl.semaphore_wait(barrier, n - 1 + above + below)
    start_all(*forward, 0)
    for step in range(1, chunks):
        pack(step)
        start_all(*forward, step)

    for param in params:
        param.wait()

    up = pltpu.make_async_remote_copy(
        src_ref=first.at[pl.ds(REACH, REACH)],
        dst_ref=halo.at[1],
        send_sem=halo_send.at[0], recv_sem=halo_recv.at[1],
        device_id=beside(-1),
        device_id_type=pl.DeviceIdType.MESH,
    )
    down = pltpu.make_async_remote_copy(
        src_ref=first.at[pl.ds(rows, REACH)],
        dst_ref=halo.at[0],
        send_sem=halo_send.at[1], recv_sem=halo_recv.at[0],
        device_id=beside(1),
        device_id_type=pl.DeviceIdType.MESH,
    )
    has_up, has_down = part > 0, part < parts_all - 1

    def send_edges(low, high):
        @pl.when(jnp.logical_and(low, has_up))
        def _():
            up.start()

        @pl.when(jnp.logical_and(high, has_down))
        def _():
            down.start()

    def take_edges(low, high):
        @pl.when(jnp.logical_and(low, has_up))
        def _():
            down.wait_recv()
            first[pl.ds(0, REACH)] = halo[0]

        @pl.when(jnp.logical_and(high, has_down))
        def _():
            up.wait_recv()
            first[pl.ds(REACH + rows, REACH)] = halo[1]

    backwards = jnp.logical_not(forwards)

    def turned_rows(places, fields, followings):
        offsets = [lon_off[level, base + row] for row in places]
        weights = [[lon_w[k, level, base + row] for k in range(4)] for row in places]
        return circled(fields, followings, offsets, weights, per, spin)

    def along(step):
        def some(t, carry):
            start = chunk_at(step) * piece + t * tile_rows
            places = [start + u for u in range(tile_rows)]
            tile = pl.multiple_of(start, tile_rows)
            recv[pl.ds(n * slot + tile, tile_rows), :] = recv[pl.ds(tile, tile_rows), :]
            fields = [recv[pl.ds(row, n, stride=slot), :] for row in places]
            followings = [recv[pl.ds(slot + row, n, stride=slot), :] for row in places]
            for row, result in zip(places, turned_rows(places, fields, followings)):
                first[REACH + row] = result
            return carry

        lax.fori_loop(0, piece // tile_rows, some, 0)

    first_row = part * rows

    def across_and_along(step):
        def some(t, carry):
            start = chunk_at(step) * piece + t * tile_rows
            places = [start + u for u in range(tile_rows)]
            fields = []
            for row in places:
                shift = lat_off[level, base + row]
                field = None
                for k in range(4):
                    source = jnp.clip(first_row + row - shift + (k - 1), 0, parts_all * rows - 1)
                    term = lat_w[k, level, base + row] * first[source - first_row + REACH]
                    field = term if field is None else field + term
                fields.append(field)
            followings = [pltpu.roll(field, n - 1, 0) for field in fields]
            for row, result in zip(places, turned_rows(places, fields, followings)):
                back[pl.ds(row, n, stride=slot), :] = result
            return carry

        lax.fori_loop(0, piece // tile_rows, some, 0)

    for step in range(chunks):
        wait_bytes(recv, recv_sem.at[step], n * piece)
        along(step)
        if chunks == 1:
            send_edges(True, True)
        elif step == 0:
            send_edges(forwards, backwards)
        elif step == chunks - 1:
            send_edges(backwards, forwards)
        if step:
            if step == 1:
                take_edges(forwards, backwards)
            across_and_along(step - 1)
            start_all(*backward, step - 1)
    if chunks == 1:
        take_edges(True, True)
    else:
        take_edges(backwards, forwards)
    across_and_along(chunks - 1)
    start_all(*backward, chunks - 1)

    for step in range(chunks):
        wait_bytes(home, home_sem.at[step], n * piece)
        for s in range(split):

            def unpack(t, carry):
                row = chunk_at(step) * piece + t * tile_rows
                start = (s * rows + row) * groups
                parts = [
                    home[pl.ds(pl.multiple_of((g * split + s) * slot + row, tile_rows), tile_rows), :]
                    for g in range(groups)
                ]
                for i, part_block in enumerate(turned(parts, per)):
                    out_ref[pl.ds(start + i, tile_rows, stride=groups), :] = part_block
                return carry

            lax.fori_loop(0, piece // tile_rows, unpack, 0)

    wait_bytes(send, send_sem, (n - 1) * rows)
    wait_bytes(back, back_sem, (n - 1) * rows)

    @pl.when(has_up)
    def _():
        up.wait_send()

    @pl.when(has_down)
    def _():
        down.wait_send()


def per_device(tracers, lon_offset, lon_weights, lat_offset, lat_weights):
    rows, width, columns = tracers.shape
    n, bands = lax.axis_size("lon"), lax.axis_size("band")
    groups = width
    per = columns // groups
    levels = lon_offset.shape[1]
    per_level = columns // levels
    split = n // groups
    assert n % groups == 0 and rows % split == 0 and per_level % per == 0
    share = rows // split
    piece = PIECE if share % PIECE == 0 else share
    chunks = share // piece
    slot = -(-share // SUB) * SUB
    flat = pltpu.VMEM((n * slot, columns), jnp.float32)
    whole = pltpu.VMEM((rows * width, columns), jnp.float32)
    dma = pltpu.SemaphoreType.DMA
    out = pl.pallas_call(
        functools.partial(kernel, n, bands, groups, share, piece, per, per_level),
        out_shape=whole,
        in_specs=[pl.BlockSpec(memory_space=pl.ANY)] * 5,
        out_specs=pl.BlockSpec(memory_space=pltpu.VMEM),
        scratch_shapes=[
            whole,
            pltpu.SMEM((levels, rows), jnp.int32),
            pltpu.SMEM((4, levels, rows), jnp.float32),
            pltpu.SMEM((levels, rows), jnp.int32),
            pltpu.SMEM((4, levels, rows), jnp.float32),
            flat,
            pltpu.VMEM(((n + 1) * slot, columns), jnp.float32),
            pltpu.VMEM((share + 2 * REACH, n, columns), jnp.float32),
            flat,
            flat,
            pltpu.VMEM((2, REACH, n, columns), jnp.float32),
            pltpu.VMEM((SUB * 2 * n, columns), jnp.float32),
            dma((chunks, split)),
            dma((4,)),
            dma,
            dma((chunks,)),
            dma,
            dma((chunks,)),
            dma((2,)),
            dma((2,)),
        ],
        compiler_params=pltpu.CompilerParams(collective_id=0, has_side_effects=True),
    )(
        tracers.reshape(rows * width, columns),
        lon_offset.T,
        lon_weights.transpose(0, 2, 1),
        lat_offset.T,
        lat_weights.transpose(0, 2, 1),
    )
    return out.reshape(rows, width, columns)


def solution(mesh):
    return jax.shard_map(
        per_device,
        mesh=mesh,
        in_specs=(
            P("band", "lon", None),
            P("band", None),
            P(None, "band", None),
            P("band", None),
            P(None, "band", None),
        ),
        out_specs=P("band", "lon", None),
        check_vma=False,
    )
```

```python
import functools
import math

import jax
import jax.numpy as jnp
from jax import lax
from jax.experimental import pallas as pl
from jax.experimental.pallas import tpu as pltpu
from jax.sharding import PartitionSpec as P

TMAX = 6
REACH = TMAX + 2
SUB = 8
PIECE = 8


def turned(parts, per):
    parts = list(parts)
    count = len(parts)
    lanes = parts[0].shape[1]
    block = lax.broadcasted_iota(jnp.int32, parts[0].shape, 1) // per
    bit = count // 2
    while bit:
        high = (block // bit) % 2 == 1
        move = per * bit
        for i in range(count):
            if i & bit:
                continue
            a, b = parts[i], parts[i | bit]
            parts[i] = jnp.where(high, pltpu.roll(b, move, 1), a)
            parts[i | bit] = jnp.where(high, b, pltpu.roll(a, lanes - move, 1))
        bit //= 2
    return parts


def circled(fields, followings, offsets, weights, per, spin):
    count, lanes = fields[0].shape
    lane = lax.broadcasted_iota(jnp.int32, fields[0].shape, 1)
    turns = []
    for u, (field, following) in enumerate(zip(fields, followings)):
        total = weights[u][0] * field
        for k in range(1, 4):
            mixed = jnp.where(lane >= per * k, field, following)
            total = total + weights[u][k] * pltpu.roll(mixed, lanes - per * k, 1)
        shift = ((offsets[u] + 1) * per + count * lanes) % (count * lanes)
        coarse, fine = shift // lanes, shift % lanes
        total = pltpu.roll(total, fine, 1)
        spin[pl.ds(2 * u * count, count), :] = total
        spin[pl.ds((2 * u + 1) * count, count), :] = total
        turns.append((coarse, fine))
    results = []
    for u, (coarse, fine) in enumerate(turns):
        near = spin[pl.ds((2 * u + 1) * count - coarse, count), :]
        far = spin[pl.ds((2 * u + 1) * count - 1 - coarse, count), :]
        results.append(jnp.where(lane >= fine, near, far))
    return results


def kernel(
    n, bands, groups, rows, piece, per, per_level,
    x_hbm, lon_off_hbm, lon_w_hbm, lat_off_hbm, lat_w_hbm, out_ref,
    x_ref, lon_off, lon_w, lat_off, lat_w,
    send, recv, first, back, home, halo, spin,
    in_sem, param_sem, send_sem, recv_sem, back_sem, home_sem, halo_send, halo_recv,
):
    me = lax.axis_index("lon")
    band = lax.axis_index("band")
    split = n // groups
    group, share = me // split, me % split
    part = band * split + share
    parts_all = bands * split
    level = group * per // per_level
    chunks = rows // piece
    tile_rows = math.gcd(SUB, piece)
    slot = send.shape[0] // n
    block = piece * groups
    mirrored = band % 2 == 1
    arrivals = [chunks - 1] + list(range(chunks - 1))
    base = share * rows

    def chunk_at(step):
        return jnp.where(mirrored, chunks - 1 - step, step)

    def fetch(step, s):
        place = pl.ds(pl.multiple_of((s * rows + chunk_at(step) * piece) * groups, SUB), block)
        return pltpu.make_async_copy(x_hbm.at[place, :], x_ref.at[place, :], in_sem.at[step, s])

    for s in range(split):
        fetch(arrivals[0], s).start()
    params = [
        pltpu.make_async_copy(source, target, param_sem.at[i])
        for i, (source, target) in enumerate(
            ((lon_off_hbm, lon_off), (lon_w_hbm, lon_w), (lat_off_hbm, lat_off), (lat_w_hbm, lat_w))
        )
    ]
    barrier = pltpu.get_barrier_semaphore()

    def greet(d, carry):
        pl.semaphore_signal(
            barrier, inc=1, device_id={"lon": lax.rem(me + d, n)},
            device_id_type=pl.DeviceIdType.MESH,
        )
        return carry

    lax.fori_loop(1, n, greet, 0)

    def beside(step):
        other = lax.rem(part + step + parts_all, parts_all)
        return {"band": other // split, "lon": group * split + other % split}

    @pl.when(part > 0)
    def _():
        pl.semaphore_signal(
            barrier, inc=1, device_id=beside(-1), device_id_type=pl.DeviceIdType.MESH
        )

    @pl.when(part < parts_all - 1)
    def _():
        pl.semaphore_signal(
            barrier, inc=1, device_id=beside(1), device_id_type=pl.DeviceIdType.MESH
        )

    for step in arrivals[1:]:
        for s in range(split):
            fetch(step, s).start()
    for param in params:
        param.start()

    def pack(step):
        for s in range(split):
            fetch(step, s).wait()

            def tile(t, carry):
                row = chunk_at(step) * piece + t * tile_rows
                start = (s * rows + row) * groups
                parts = [
                    x_ref[pl.ds(start + i, tile_rows, stride=groups), :] for i in range(groups)
                ]
                for g, part_block in enumerate(turned(parts, per)):
                    to = (g * split + s) * slot + row
                    send[pl.ds(pl.multiple_of(to, tile_rows), tile_rows), :] = part_block
                return carry

            lax.fori_loop(0, piece // tile_rows, tile, 0)

    def place_of(peer, step):
        return pl.ds(pl.multiple_of(peer * slot + chunk_at(step) * piece, SUB), piece)

    def start_all(source, target, s_sem, r_sem, step):
        def one(i, carry):
            peer = lax.rem(me + i // 2 + jnp.where(i % 2 == 0, n // 2, 1), n)
            pltpu.make_async_remote_copy(
                src_ref=source.at[place_of(peer, step), :],
                dst_ref=target.at[place_of(me, step), :],
                send_sem=s_sem,
                recv_sem=r_sem.at[step],
                device_id={"lon": peer},
                device_id_type=pl.DeviceIdType.MESH,
            ).start()
            return carry

        place = place_of(me, step)
        pltpu.make_async_copy(source.at[place, :], target.at[place, :], r_sem.at[step]).start()
        lax.fori_loop(0, n - 1, one, 0)

    def wait_bytes(ref, sem, count):
        whole = ref.at[pl.ds(0, count), :]
        pltpu.make_async_copy(whole, whole, sem).wait()

    forward = (send, recv, send_sem, recv_sem)
    backward = (back, home, back_sem, home_sem)

    pack(arrivals[0])
    above = jnp.where(part > 0, 1, 0)
    below = jnp.where(part < parts_all - 1, 1, 0)
    pl.semaphore_wait(barrier, n - 1 + above + below)
    start_all(*forward, arrivals[0])
    for step in arrivals[1:]:
        pack(step)
        start_all(*forward, step)

    for param in params:
        param.wait()

    up = pltpu.make_async_remote_copy(
        src_ref=first.at[pl.ds(REACH, REACH)],
        dst_ref=halo.at[1],
        send_sem=halo_send.at[0], recv_sem=halo_recv.at[1],
        device_id=beside(-1),
        device_id_type=pl.DeviceIdType.MESH,
    )
    down = pltpu.make_async_remote_copy(
        src_ref=first.at[pl.ds(rows, REACH)],
        dst_ref=halo.at[0],
        send_sem=halo_send.at[1], recv_sem=halo_recv.at[0],
        device_id=beside(1),
        device_id_type=pl.DeviceIdType.MESH,
    )
    has_up, has_down = part > 0, part < parts_all - 1

    def send_edges(low, high):
        @pl.when(jnp.logical_and(low, has_up))
        def _():
            up.start()

        @pl.when(jnp.logical_and(high, has_down))
        def _():
            down.start()

    def take_edges(low, high):
        @pl.when(jnp.logical_and(low, has_up))
        def _():
            down.wait_recv()
            first[pl.ds(0, REACH)] = halo[0]

        @pl.when(jnp.logical_and(high, has_down))
        def _():
            up.wait_recv()
            first[pl.ds(REACH + rows, REACH)] = halo[1]

    plain = jnp.logical_not(mirrored)

    def turned_rows(places, fields, followings):
        offsets = [lon_off[level, base + row] for row in places]
        weights = [[lon_w[k, level, base + row] for k in range(4)] for row in places]
        return circled(fields, followings, offsets, weights, per, spin)

    def along(step):
        def some(t, carry):
            start = chunk_at(step) * piece + t * tile_rows
            places = [start + u for u in range(tile_rows)]
            tile = pl.multiple_of(start, tile_rows)
            recv[pl.ds(n * slot + tile, tile_rows), :] = recv[pl.ds(tile, tile_rows), :]
            fields = [recv[pl.ds(row, n, stride=slot), :] for row in places]
            followings = [recv[pl.ds(slot + row, n, stride=slot), :] for row in places]
            for row, result in zip(places, turned_rows(places, fields, followings)):
                first[REACH + row] = result
            return carry

        lax.fori_loop(0, piece // tile_rows, some, 0)

    first_row = part * rows

    def across_and_along(step):
        def some(t, carry):
            start = chunk_at(step) * piece + t * tile_rows
            places = [start + u for u in range(tile_rows)]
            fields = []
            for row in places:
                shift = lat_off[level, base + row]
                field = None
                for k in range(4):
                    source = jnp.clip(first_row + row - shift + (k - 1), 0, parts_all * rows - 1)
                    term = lat_w[k, level, base + row] * first[source - first_row + REACH]
                    field = term if field is None else field + term
                fields.append(field)
            followings = [pltpu.roll(field, n - 1, 0) for field in fields]
            for row, result in zip(places, turned_rows(places, fields, followings)):
                back[pl.ds(row, n, stride=slot), :] = result
            return carry

        lax.fori_loop(0, piece // tile_rows, some, 0)

    for place, step in enumerate(arrivals):
        wait_bytes(recv, recv_sem.at[step], n * piece)
        along(step)
        if step == chunks - 1:
            send_edges(mirrored, plain)
        if step == 0:
            send_edges(plain, mirrored)
        if place >= 2:
            if step == 1:
                take_edges(plain, mirrored)
            across_and_along(step - 1)
            start_all(*backward, step - 1)
    if chunks < 3:
        take_edges(plain, mirrored)
    if chunks > 1:
        across_and_along(chunks - 2)
        start_all(*backward, chunks - 2)
    take_edges(mirrored, plain)
    across_and_along(chunks - 1)
    start_all(*backward, chunks - 1)

    for step in range(chunks):
        wait_bytes(home, home_sem.at[step], n * piece)
        for s in range(split):

            def unpack(t, carry):
                row = chunk_at(step) * piece + t * tile_rows
                start = (s * rows + row) * groups
                parts = [
                    home[pl.ds(pl.multiple_of((g * split + s) * slot + row, tile_rows), tile_rows), :]
                    for g in range(groups)
                ]
                for i, part_block in enumerate(turned(parts, per)):
                    out_ref[pl.ds(start + i, tile_rows, stride=groups), :] = part_block
                return carry

            lax.fori_loop(0, piece // tile_rows, unpack, 0)

    wait_bytes(send, send_sem, (n - 1) * rows)
    wait_bytes(back, back_sem, (n - 1) * rows)

    @pl.when(has_up)
    def _():
        up.wait_send()

    @pl.when(has_down)
    def _():
        down.wait_send()


def per_device(tracers, lon_offset, lon_weights, lat_offset, lat_weights):
    rows, width, columns = tracers.shape
    n, bands = lax.axis_size("lon"), lax.axis_size("band")
    groups = width
    per = columns // groups
    levels = lon_offset.shape[1]
    per_level = columns // levels
    split = n // groups
    assert n % groups == 0 and rows % split == 0 and per_level % per == 0
    share = rows // split
    piece = PIECE if share % PIECE == 0 else share
    chunks = share // piece
    slot = -(-share // SUB) * SUB
    flat = pltpu.VMEM((n * slot, columns), jnp.float32)
    whole = pltpu.VMEM((rows * width, columns), jnp.float32)
    dma = pltpu.SemaphoreType.DMA
    out = pl.pallas_call(
        functools.partial(kernel, n, bands, groups, share, piece, per, per_level),
        out_shape=whole,
        in_specs=[pl.BlockSpec(memory_space=pl.ANY)] * 5,
        out_specs=pl.BlockSpec(memory_space=pltpu.VMEM),
        scratch_shapes=[
            whole,
            pltpu.SMEM((levels, rows), jnp.int32),
            pltpu.SMEM((4, levels, rows), jnp.float32),
            pltpu.SMEM((levels, rows), jnp.int32),
            pltpu.SMEM((4, levels, rows), jnp.float32),
            flat,
            pltpu.VMEM(((n + 1) * slot, columns), jnp.float32),
            pltpu.VMEM((share + 2 * REACH, n, columns), jnp.float32),
            flat,
            flat,
            pltpu.VMEM((2, REACH, n, columns), jnp.float32),
            pltpu.VMEM((SUB * 2 * n, columns), jnp.float32),
            dma((chunks, split)),
            dma((4,)),
            dma,
            dma((chunks,)),
            dma,
            dma((chunks,)),
            dma((2,)),
            dma((2,)),
        ],
        compiler_params=pltpu.CompilerParams(collective_id=0, has_side_effects=True),
    )(
        tracers.reshape(rows * width, columns),
        lon_offset.T,
        lon_weights.transpose(0, 2, 1),
        lat_offset.T,
        lat_weights.transpose(0, 2, 1),
    )
    return out.reshape(rows, width, columns)


def solution(mesh):
    return jax.shard_map(
        per_device,
        mesh=mesh,
        in_specs=(
            P("band", "lon", None),
            P("band", None),
            P(None, "band", None),
            P("band", None),
            P(None, "band", None),
        ),
        out_specs=P("band", "lon", None),
        check_vma=False,
    )
```

```python
import functools
import math

import jax
import jax.numpy as jnp
from jax import lax
from jax.experimental import pallas as pl
from jax.experimental.pallas import tpu as pltpu
from jax.sharding import PartitionSpec as P

TMAX = 6
REACH = TMAX + 2
SUB = 8
PIECE = 8
AHEAD = 3


def turned(parts, per):
    parts = list(parts)
    count = len(parts)
    lanes = parts[0].shape[1]
    block = lax.broadcasted_iota(jnp.int32, parts[0].shape, 1) // per
    bit = count // 2
    while bit:
        high = (block // bit) % 2 == 1
        move = per * bit
        for i in range(count):
            if i & bit:
                continue
            a, b = parts[i], parts[i | bit]
            parts[i] = jnp.where(high, pltpu.roll(b, move, 1), a)
            parts[i | bit] = jnp.where(high, b, pltpu.roll(a, lanes - move, 1))
        bit //= 2
    return parts


def circled(fields, followings, offsets, weights, per, spin):
    count, lanes = fields[0].shape
    lane = lax.broadcasted_iota(jnp.int32, fields[0].shape, 1)
    turns = []
    for u, (field, following) in enumerate(zip(fields, followings)):
        total = weights[u][0] * field
        for k in range(1, 4):
            mixed = jnp.where(lane >= per * k, field, following)
            total = total + weights[u][k] * pltpu.roll(mixed, lanes - per * k, 1)
        shift = ((offsets[u] + 1) * per + count * lanes) % (count * lanes)
        coarse, fine = shift // lanes, shift % lanes
        total = pltpu.roll(total, fine, 1)
        spin[pl.ds(2 * u * count, count), :] = total
        spin[pl.ds((2 * u + 1) * count, count), :] = total
        turns.append((coarse, fine))
    results = []
    for u, (coarse, fine) in enumerate(turns):
        near = spin[pl.ds((2 * u + 1) * count - coarse, count), :]
        far = spin[pl.ds((2 * u + 1) * count - 1 - coarse, count), :]
        results.append(jnp.where(lane >= fine, near, far))
    return results


def kernel(
    n, bands, groups, rows, piece, per, per_level,
    x_hbm, lon_off_hbm, lon_w_hbm, lat_off_hbm, lat_w_hbm, out_ref,
    x_ref, lon_off, lon_w, lat_off, lat_w,
    send, recv, first, back, home, halo, spin,
    in_sem, param_sem, send_sem, recv_sem, back_sem, home_sem, halo_send, halo_recv,
):
    me = lax.axis_index("lon")
    band = lax.axis_index("band")
    split = n // groups
    group, share = me // split, me % split
    part = band * split + share
    parts_all = bands * split
    level = group * per // per_level
    chunks = rows // piece
    tile_rows = math.gcd(SUB, piece)
    slot = send.shape[0] // n
    block = piece * groups
    mirrored = band % 2 == 1
    arrivals = [chunks - 1] + list(range(chunks - 1))
    base = share * rows

    def chunk_at(step):
        return jnp.where(mirrored, chunks - 1 - step, step)

    def fetch(step, s):
        place = pl.ds(pl.multiple_of((s * rows + chunk_at(step) * piece) * groups, SUB), block)
        return pltpu.make_async_copy(x_hbm.at[place, :], x_ref.at[place, :], in_sem.at[step, s])

    for s in range(split):
        fetch(arrivals[0], s).start()
    params = [
        pltpu.make_async_copy(source, target, param_sem.at[i])
        for i, (source, target) in enumerate(
            ((lon_off_hbm, lon_off), (lon_w_hbm, lon_w), (lat_off_hbm, lat_off), (lat_w_hbm, lat_w))
        )
    ]
    barrier = pltpu.get_barrier_semaphore()

    def greet(d, carry):
        pl.semaphore_signal(
            barrier, inc=1, device_id={"lon": lax.rem(me + d, n)},
            device_id_type=pl.DeviceIdType.MESH,
        )
        return carry

    lax.fori_loop(1, n, greet, 0)

    def beside(step):
        other = lax.rem(part + step + parts_all, parts_all)
        return {"band": other // split, "lon": group * split + other % split}

    @pl.when(part > 0)
    def _():
        pl.semaphore_signal(
            barrier, inc=1, device_id=beside(-1), device_id_type=pl.DeviceIdType.MESH
        )

    @pl.when(part < parts_all - 1)
    def _():
        pl.semaphore_signal(
            barrier, inc=1, device_id=beside(1), device_id_type=pl.DeviceIdType.MESH
        )

    for step in arrivals[1:]:
        for s in range(split):
            fetch(step, s).start()
    for param in params:
        param.start()

    def pack(step):
        for s in range(split):
            fetch(step, s).wait()

            def tile(t, carry):
                row = chunk_at(step) * piece + t * tile_rows
                start = (s * rows + row) * groups
                parts = [
                    x_ref[pl.ds(start + i, tile_rows, stride=groups), :] for i in range(groups)
                ]
                for g, part_block in enumerate(turned(parts, per)):
                    to = (g * split + s) * slot + row
                    send[pl.ds(pl.multiple_of(to, tile_rows), tile_rows), :] = part_block
                return carry

            lax.fori_loop(0, piece // tile_rows, tile, 0)

    def place_of(peer, step):
        return pl.ds(pl.multiple_of(peer * slot + chunk_at(step) * piece, SUB), piece)

    def start_all(source, target, s_sem, r_sem, step):
        def one(i, carry):
            peer = lax.rem(me + i // 2 + jnp.where(i % 2 == 0, n // 2, 1), n)
            pltpu.make_async_remote_copy(
                src_ref=source.at[place_of(peer, step), :],
                dst_ref=target.at[place_of(me, step), :],
                send_sem=s_sem,
                recv_sem=r_sem.at[step],
                device_id={"lon": peer},
                device_id_type=pl.DeviceIdType.MESH,
            ).start()
            return carry

        place = place_of(me, step)
        pltpu.make_async_copy(source.at[place, :], target.at[place, :], r_sem.at[step]).start()
        lax.fori_loop(0, n - 1, one, 0)

    def wait_bytes(ref, sem, count):
        whole = ref.at[pl.ds(0, count), :]
        pltpu.make_async_copy(whole, whole, sem).wait()

    forward = (send, recv, send_sem, recv_sem)
    backward = (back, home, back_sem, home_sem)

    pack(arrivals[0])
    above = jnp.where(part > 0, 1, 0)
    below = jnp.where(part < parts_all - 1, 1, 0)
    pl.semaphore_wait(barrier, n - 1 + above + below)
    start_all(*forward, arrivals[0])
    for place, step in enumerate(arrivals[1:], 1):
        pack(step)
        if place < AHEAD:
            start_all(*forward, step)

    for param in params:
        param.wait()

    up = pltpu.make_async_remote_copy(
        src_ref=first.at[pl.ds(REACH, REACH)],
        dst_ref=halo.at[1],
        send_sem=halo_send.at[0], recv_sem=halo_recv.at[1],
        device_id=beside(-1),
        device_id_type=pl.DeviceIdType.MESH,
    )
    down = pltpu.make_async_remote_copy(
        src_ref=first.at[pl.ds(rows, REACH)],
        dst_ref=halo.at[0],
        send_sem=halo_send.at[1], recv_sem=halo_recv.at[0],
        device_id=beside(1),
        device_id_type=pl.DeviceIdType.MESH,
    )
    has_up, has_down = part > 0, part < parts_all - 1

    def send_edges(low, high):
        @pl.when(jnp.logical_and(low, has_up))
        def _():
            up.start()

        @pl.when(jnp.logical_and(high, has_down))
        def _():
            down.start()

    def take_edges(low, high):
        @pl.when(jnp.logical_and(low, has_up))
        def _():
            down.wait_recv()
            first[pl.ds(0, REACH)] = halo[0]

        @pl.when(jnp.logical_and(high, has_down))
        def _():
            up.wait_recv()
            first[pl.ds(REACH + rows, REACH)] = halo[1]

    plain = jnp.logical_not(mirrored)

    def turned_rows(places, fields, followings):
        offsets = [lon_off[level, base + row] for row in places]
        weights = [[lon_w[k, level, base + row] for k in range(4)] for row in places]
        return circled(fields, followings, offsets, weights, per, spin)

    def along(step):
        def some(t, carry):
            start = chunk_at(step) * piece + t * tile_rows
            places = [start + u for u in range(tile_rows)]
            tile = pl.multiple_of(start, tile_rows)
            recv[pl.ds(n * slot + tile, tile_rows), :] = recv[pl.ds(tile, tile_rows), :]
            fields = [recv[pl.ds(row, n, stride=slot), :] for row in places]
            followings = [recv[pl.ds(slot + row, n, stride=slot), :] for row in places]
            for row, result in zip(places, turned_rows(places, fields, followings)):
                first[REACH + row] = result
            return carry

        lax.fori_loop(0, piece // tile_rows, some, 0)

    first_row = part * rows

    def across_and_along(step):
        def some(t, carry):
            start = chunk_at(step) * piece + t * tile_rows
            places = [start + u for u in range(tile_rows)]
            fields = []
            for row in places:
                shift = lat_off[level, base + row]
                field = None
                for k in range(4):
                    source = jnp.clip(first_row + row - shift + (k - 1), 0, parts_all * rows - 1)
                    term = lat_w[k, level, base + row] * first[source - first_row + REACH]
                    field = term if field is None else field + term
                fields.append(field)
            followings = [pltpu.roll(field, n - 1, 0) for field in fields]
            for row, result in zip(places, turned_rows(places, fields, followings)):
                back[pl.ds(row, n, stride=slot), :] = result
            return carry

        lax.fori_loop(0, piece // tile_rows, some, 0)

    for place, step in enumerate(arrivals):
        wait_bytes(recv, recv_sem.at[step], n * piece)
        if place + AHEAD < chunks:
            start_all(*forward, arrivals[place + AHEAD])
        along(step)
        if step == chunks - 1:
            send_edges(mirrored, plain)
        if step == 0:
            send_edges(plain, mirrored)
        if place >= 2:
            if step == 1:
                take_edges(plain, mirrored)
            across_and_along(step - 1)
            start_all(*backward, step - 1)
    if chunks < 3:
        take_edges(plain, mirrored)
    if chunks > 1:
        across_and_along(chunks - 2)
        start_all(*backward, chunks - 2)
    take_edges(mirrored, plain)
    across_and_along(chunks - 1)
    start_all(*backward, chunks - 1)

    for step in range(chunks):
        wait_bytes(home, home_sem.at[step], n * piece)
        for s in range(split):

            def unpack(t, carry):
                row = chunk_at(step) * piece + t * tile_rows
                start = (s * rows + row) * groups
                parts = [
                    home[pl.ds(pl.multiple_of((g * split + s) * slot + row, tile_rows), tile_rows), :]
                    for g in range(groups)
                ]
                for i, part_block in enumerate(turned(parts, per)):
                    out_ref[pl.ds(start + i, tile_rows, stride=groups), :] = part_block
                return carry

            lax.fori_loop(0, piece // tile_rows, unpack, 0)

    wait_bytes(send, send_sem, (n - 1) * rows)
    wait_bytes(back, back_sem, (n - 1) * rows)

    @pl.when(has_up)
    def _():
        up.wait_send()

    @pl.when(has_down)
    def _():
        down.wait_send()


def per_device(tracers, lon_offset, lon_weights, lat_offset, lat_weights):
    rows, width, columns = tracers.shape
    n, bands = lax.axis_size("lon"), lax.axis_size("band")
    groups = width
    per = columns // groups
    levels = lon_offset.shape[1]
    per_level = columns // levels
    split = n // groups
    assert n % groups == 0 and rows % split == 0 and per_level % per == 0
    share = rows // split
    piece = PIECE if share % PIECE == 0 else share
    chunks = share // piece
    slot = -(-share // SUB) * SUB
    flat = pltpu.VMEM((n * slot, columns), jnp.float32)
    whole = pltpu.VMEM((rows * width, columns), jnp.float32)
    dma = pltpu.SemaphoreType.DMA
    out = pl.pallas_call(
        functools.partial(kernel, n, bands, groups, share, piece, per, per_level),
        out_shape=whole,
        in_specs=[pl.BlockSpec(memory_space=pl.ANY)] * 5,
        out_specs=pl.BlockSpec(memory_space=pltpu.VMEM),
        scratch_shapes=[
            whole,
            pltpu.SMEM((levels, rows), jnp.int32),
            pltpu.SMEM((4, levels, rows), jnp.float32),
            pltpu.SMEM((levels, rows), jnp.int32),
            pltpu.SMEM((4, levels, rows), jnp.float32),
            flat,
            pltpu.VMEM(((n + 1) * slot, columns), jnp.float32),
            pltpu.VMEM((share + 2 * REACH, n, columns), jnp.float32),
            flat,
            flat,
            pltpu.VMEM((2, REACH, n, columns), jnp.float32),
            pltpu.VMEM((SUB * 2 * n, columns), jnp.float32),
            dma((chunks, split)),
            dma((4,)),
            dma,
            dma((chunks,)),
            dma,
            dma((chunks,)),
            dma((2,)),
            dma((2,)),
        ],
        compiler_params=pltpu.CompilerParams(collective_id=0, has_side_effects=True),
    )(
        tracers.reshape(rows * width, columns),
        lon_offset.T,
        lon_weights.transpose(0, 2, 1),
        lat_offset.T,
        lat_weights.transpose(0, 2, 1),
    )
    return out.reshape(rows, width, columns)


def solution(mesh):
    return jax.shard_map(
        per_device,
        mesh=mesh,
        in_specs=(
            P("band", "lon", None),
            P("band", None),
            P(None, "band", None),
            P("band", None),
            P(None, "band", None),
        ),
        out_specs=P("band", "lon", None),
        check_vma=False,
    )
```

```python
import functools
import math

import jax
import jax.numpy as jnp
from jax import lax
from jax.experimental import pallas as pl
from jax.experimental.pallas import tpu as pltpu
from jax.sharding import PartitionSpec as P

TMAX = 6
REACH = TMAX + 2
SUB = 8
PIECE = 8


def turned(parts, per):
    parts = list(parts)
    count = len(parts)
    lanes = parts[0].shape[1]
    block = lax.broadcasted_iota(jnp.int32, parts[0].shape, 1) // per
    bit = count // 2
    while bit:
        high = (block // bit) % 2 == 1
        move = per * bit
        for i in range(count):
            if i & bit:
                continue
            a, b = parts[i], parts[i | bit]
            parts[i] = jnp.where(high, pltpu.roll(b, move, 1), a)
            parts[i | bit] = jnp.where(high, b, pltpu.roll(a, lanes - move, 1))
        bit //= 2
    return parts


def circled(fields, followings, offsets, weights, per, spin):
    count, lanes = fields[0].shape
    lane = lax.broadcasted_iota(jnp.int32, fields[0].shape, 1)
    turns = []
    for u, (field, following) in enumerate(zip(fields, followings)):
        total = weights[u][0] * field
        for k in range(1, 4):
            mixed = jnp.where(lane >= per * k, field, following)
            total = total + weights[u][k] * pltpu.roll(mixed, lanes - per * k, 1)
        shift = ((offsets[u] + 1) * per + count * lanes) % (count * lanes)
        coarse, fine = shift // lanes, shift % lanes
        total = pltpu.roll(total, fine, 1)
        spin[pl.ds(2 * u * count, count), :] = total
        spin[pl.ds((2 * u + 1) * count, count), :] = total
        turns.append((coarse, fine))
    results = []
    for u, (coarse, fine) in enumerate(turns):
        near = spin[pl.ds((2 * u + 1) * count - coarse, count), :]
        far = spin[pl.ds((2 * u + 1) * count - 1 - coarse, count), :]
        results.append(jnp.where(lane >= fine, near, far))
    return results


def kernel(
    n, bands, groups, rows, piece, per, per_level,
    x_hbm, lon_off_hbm, lon_w_hbm, lat_off_hbm, lat_w_hbm, out_ref,
    x_ref, lon_off, lon_w, lat_off, lat_w,
    send, recv, first, back, home, halo, spin,
    in_sem, param_sem, send_sem, recv_sem, back_sem, home_sem, halo_send, halo_recv,
):
    me = lax.axis_index("lon")
    band = lax.axis_index("band")
    split = n // groups
    group, share = me // split, me % split
    part = band * split + share
    parts_all = bands * split
    level = group * per // per_level
    chunks = rows // piece
    tile_rows = math.gcd(SUB, piece)
    slot = send.shape[0] // n
    block = piece * groups
    forwards = band % 2 == 1
    base = share * rows

    def chunk_at(step):
        return jnp.where(forwards, step, chunks - 1 - step)

    def fetch(step, s):
        place = pl.ds(pl.multiple_of((s * rows + chunk_at(step) * piece) * groups, SUB), block)
        return pltpu.make_async_copy(x_hbm.at[place, :], x_ref.at[place, :], in_sem.at[step, s])

    for s in range(split):
        fetch(0, s).start()
    params = [
        pltpu.make_async_copy(source, target, param_sem.at[i])
        for i, (source, target) in enumerate(
            ((lon_off_hbm, lon_off), (lon_w_hbm, lon_w), (lat_off_hbm, lat_off), (lat_w_hbm, lat_w))
        )
    ]
    barrier = pltpu.get_barrier_semaphore()

    distances = [i // 2 + (1 if i % 2 else n // 2) for i in range(n - 1)]

    def peer_at(d):
        return jnp.where(me + d >= n, me + d - n, me + d)

    for d in distances:
        pl.semaphore_signal(
            barrier, inc=1, device_id={"lon": peer_at(d)}, device_id_type=pl.DeviceIdType.MESH
        )

    def beside(step):
        other = lax.rem(part + step + parts_all, parts_all)
        return {"band": other // split, "lon": group * split + other % split}

    @pl.when(part > 0)
    def _():
        pl.semaphore_signal(
            barrier, inc=1, device_id=beside(-1), device_id_type=pl.DeviceIdType.MESH
        )

    @pl.when(part < parts_all - 1)
    def _():
        pl.semaphore_signal(
            barrier, inc=1, device_id=beside(1), device_id_type=pl.DeviceIdType.MESH
        )

    for step in range(1, chunks):
        for s in range(split):
            fetch(step, s).start()
    for param in params:
        param.start()

    def pack(step):
        for s in range(split):
            fetch(step, s).wait()

            def tile(t, carry):
                row = chunk_at(step) * piece + t * tile_rows
                start = (s * rows + row) * groups
                parts = [
                    x_ref[pl.ds(start + i, tile_rows, stride=groups), :] for i in range(groups)
                ]
                for g, part_block in enumerate(turned(parts, per)):
                    to = (g * split + s) * slot + row
                    send[pl.ds(pl.multiple_of(to, tile_rows), tile_rows), :] = part_block
                return carry

            lax.fori_loop(0, piece // tile_rows, tile, 0)

    def place_of(peer, step):
        return pl.ds(pl.multiple_of(peer * slot + chunk_at(step) * piece, SUB), piece)

    def start_all(source, target, s_sem, r_sem, step):
        place = place_of(me, step)
        pltpu.make_async_copy(source.at[place, :], target.at[place, :], r_sem.at[step]).start()
        for d in distances:
            pltpu.make_async_remote_copy(
                src_ref=source.at[place_of(peer_at(d), step), :],
                dst_ref=target.at[place, :],
                send_sem=s_sem,
                recv_sem=r_sem.at[step],
                device_id={"lon": peer_at(d)},
                device_id_type=pl.DeviceIdType.MESH,
            ).start()

    def wait_bytes(ref, sem, count):
        whole = ref.at[pl.ds(0, count), :]
        pltpu.make_async_copy(whole, whole, sem).wait()

    forward = (send, recv, send_sem, recv_sem)
    backward = (back, home, back_sem, home_sem)

    pack(0)
    above = jnp.where(part > 0, 1, 0)
    below = jnp.where(part < parts_all - 1, 1, 0)
    pl.semaphore_wait(barrier, n - 1 + above + below)
    start_all(*forward, 0)
    for step in range(1, chunks):
        pack(step)
        start_all(*forward, step)

    for param in params:
        param.wait()

    up = pltpu.make_async_remote_copy(
        src_ref=first.at[pl.ds(REACH, REACH)],
        dst_ref=halo.at[1],
        send_sem=halo_send.at[0], recv_sem=halo_recv.at[1],
        device_id=beside(-1),
        device_id_type=pl.DeviceIdType.MESH,
    )
    down = pltpu.make_async_remote_copy(
        src_ref=first.at[pl.ds(rows, REACH)],
        dst_ref=halo.at[0],
        send_sem=halo_send.at[1], recv_sem=halo_recv.at[0],
        device_id=beside(1),
        device_id_type=pl.DeviceIdType.MESH,
    )
    has_up, has_down = part > 0, part < parts_all - 1

    def send_edges(low, high):
        @pl.when(jnp.logical_and(low, has_up))
        def _():
            up.start()

        @pl.when(jnp.logical_and(high, has_down))
        def _():
            down.start()

    def take_edges(low, high):
        @pl.when(jnp.logical_and(low, has_up))
        def _():
            down.wait_recv()
            first[pl.ds(0, REACH)] = halo[0]

        @pl.when(jnp.logical_and(high, has_down))
        def _():
            up.wait_recv()
            first[pl.ds(REACH + rows, REACH)] = halo[1]

    backwards = jnp.logical_not(forwards)

    def turned_rows(places, fields, followings):
        offsets = [lon_off[level, base + row] for row in places]
        weights = [[lon_w[k, level, base + row] for k in range(4)] for row in places]
        return circled(fields, followings, offsets, weights, per, spin)

    def along(step):
        def some(t, carry):
            start = chunk_at(step) * piece + t * tile_rows
            places = [start + u for u in range(tile_rows)]
            tile = pl.multiple_of(start, tile_rows)
            recv[pl.ds(n * slot + tile, tile_rows), :] = recv[pl.ds(tile, tile_rows), :]
            fields = [recv[pl.ds(row, n, stride=slot), :] for row in places]
            followings = [recv[pl.ds(slot + row, n, stride=slot), :] for row in places]
            for row, result in zip(places, turned_rows(places, fields, followings)):
                first[REACH + row] = result
            return carry

        lax.fori_loop(0, piece // tile_rows, some, 0)

    first_row = part * rows

    def across_and_along(step):
        def some(t, carry):
            start = chunk_at(step) * piece + t * tile_rows
            places = [start + u for u in range(tile_rows)]
            fields = []
            for row in places:
                shift = lat_off[level, base + row]
                field = None
                for k in range(4):
                    source = jnp.clip(first_row + row - shift + (k - 1), 0, parts_all * rows - 1)
                    term = lat_w[k, level, base + row] * first[source - first_row + REACH]
                    field = term if field is None else field + term
                fields.append(field)
            followings = [pltpu.roll(field, n - 1, 0) for field in fields]
            for row, result in zip(places, turned_rows(places, fields, followings)):
                back[pl.ds(row, n, stride=slot), :] = result
            return carry

        lax.fori_loop(0, piece // tile_rows, some, 0)

    for step in range(chunks):
        wait_bytes(recv, recv_sem.at[step], n * piece)
        along(step)
        if chunks == 1:
            send_edges(True, True)
        elif step == 0:
            send_edges(forwards, backwards)
        elif step == chunks - 1:
            send_edges(backwards, forwards)
        if step:
            if step == 1:
                take_edges(forwards, backwards)
            across_and_along(step - 1)
            start_all(*backward, step - 1)
    if chunks == 1:
        take_edges(True, True)
    else:
        take_edges(backwards, forwards)
    across_and_along(chunks - 1)
    start_all(*backward, chunks - 1)

    for step in range(chunks):
        wait_bytes(home, home_sem.at[step], n * piece)
        for s in range(split):

            def unpack(t, carry):
                row = chunk_at(step) * piece + t * tile_rows
                start = (s * rows + row) * groups
                parts = [
                    home[pl.ds(pl.multiple_of((g * split + s) * slot + row, tile_rows), tile_rows), :]
                    for g in range(groups)
                ]
                for i, part_block in enumerate(turned(parts, per)):
                    out_ref[pl.ds(start + i, tile_rows, stride=groups), :] = part_block
                return carry

            lax.fori_loop(0, piece // tile_rows, unpack, 0)

    wait_bytes(send, send_sem, (n - 1) * rows)
    wait_bytes(back, back_sem, (n - 1) * rows)

    @pl.when(has_up)
    def _():
        up.wait_send()

    @pl.when(has_down)
    def _():
        down.wait_send()


def per_device(tracers, lon_offset, lon_weights, lat_offset, lat_weights):
    rows, width, columns = tracers.shape
    n, bands = lax.axis_size("lon"), lax.axis_size("band")
    groups = width
    per = columns // groups
    levels = lon_offset.shape[1]
    per_level = columns // levels
    split = n // groups
    assert n % groups == 0 and rows % split == 0 and per_level % per == 0
    share = rows // split
    piece = PIECE if share % PIECE == 0 else share
    chunks = share // piece
    slot = -(-share // SUB) * SUB
    flat = pltpu.VMEM((n * slot, columns), jnp.float32)
    whole = pltpu.VMEM((rows * width, columns), jnp.float32)
    dma = pltpu.SemaphoreType.DMA
    out = pl.pallas_call(
        functools.partial(kernel, n, bands, groups, share, piece, per, per_level),
        out_shape=whole,
        in_specs=[pl.BlockSpec(memory_space=pl.ANY)] * 5,
        out_specs=pl.BlockSpec(memory_space=pltpu.VMEM),
        scratch_shapes=[
            whole,
            pltpu.SMEM((levels, rows), jnp.int32),
            pltpu.SMEM((4, levels, rows), jnp.float32),
            pltpu.SMEM((levels, rows), jnp.int32),
            pltpu.SMEM((4, levels, rows), jnp.float32),
            flat,
            pltpu.VMEM(((n + 1) * slot, columns), jnp.float32),
            pltpu.VMEM((share + 2 * REACH, n, columns), jnp.float32),
            flat,
            flat,
            pltpu.VMEM((2, REACH, n, columns), jnp.float32),
            pltpu.VMEM((SUB * 2 * n, columns), jnp.float32),
            dma((chunks, split)),
            dma((4,)),
            dma,
            dma((chunks,)),
            dma,
            dma((chunks,)),
            dma((2,)),
            dma((2,)),
        ],
        compiler_params=pltpu.CompilerParams(collective_id=0, has_side_effects=True),
    )(
        tracers.reshape(rows * width, columns),
        lon_offset.T,
        lon_weights.transpose(0, 2, 1),
        lat_offset.T,
        lat_weights.transpose(0, 2, 1),
    )
    return out.reshape(rows, width, columns)


def solution(mesh):
    return jax.shard_map(
        per_device,
        mesh=mesh,
        in_specs=(
            P("band", "lon", None),
            P("band", None),
            P(None, "band", None),
            P("band", None),
            P(None, "band", None),
        ),
        out_specs=P("band", "lon", None),
        check_vma=False,
    )
```

```python
import functools
import math

import jax
import jax.numpy as jnp
from jax import lax
from jax.experimental import pallas as pl
from jax.experimental.pallas import tpu as pltpu
from jax.sharding import PartitionSpec as P

TMAX = 6
REACH = TMAX + 2
SUB = 8
PIECE = 8


def turned(parts, per):
    parts = list(parts)
    count = len(parts)
    lanes = parts[0].shape[1]
    block = lax.broadcasted_iota(jnp.int32, parts[0].shape, 1) // per
    bit = count // 2
    while bit:
        high = (block // bit) % 2 == 1
        move = per * bit
        for i in range(count):
            if i & bit:
                continue
            a, b = parts[i], parts[i | bit]
            parts[i] = jnp.where(high, pltpu.roll(b, move, 1), a)
            parts[i | bit] = jnp.where(high, b, pltpu.roll(a, lanes - move, 1))
        bit //= 2
    return parts


def circled(fields, followings, offsets, weights, per, spin):
    count, lanes = fields[0].shape
    lane = lax.broadcasted_iota(jnp.int32, fields[0].shape, 1)
    turns = []
    for u, (field, following) in enumerate(zip(fields, followings)):
        total = weights[u][0] * field
        for k in range(1, 4):
            mixed = jnp.where(lane >= per * k, field, following)
            total = total + weights[u][k] * pltpu.roll(mixed, lanes - per * k, 1)
        shift = ((offsets[u] + 1) * per + count * lanes) % (count * lanes)
        coarse, fine = shift // lanes, shift % lanes
        total = pltpu.roll(total, fine, 1)
        spin[pl.ds(2 * u * count, count), :] = total
        spin[pl.ds((2 * u + 1) * count, count), :] = total
        turns.append((coarse, fine))
    results = []
    for u, (coarse, fine) in enumerate(turns):
        near = spin[pl.ds((2 * u + 1) * count - coarse, count), :]
        far = spin[pl.ds((2 * u + 1) * count - 1 - coarse, count), :]
        results.append(jnp.where(lane >= fine, near, far))
    return results


def kernel(
    n, bands, groups, rows, piece, per, per_level,
    x_hbm, lon_off_hbm, lon_w_hbm, lat_off_hbm, lat_w_hbm, out_ref,
    x_ref, lon_off, lon_w, lat_off, lat_w,
    send, recv, first, back, home, halo, spin,
    in_sem, param_sem, send_sem, recv_sem, back_sem, home_sem, halo_send, halo_recv,
):
    me = lax.axis_index("lon")
    band = lax.axis_index("band")
    split = n // groups
    group, share = me // split, me % split
    part = band * split + share
    parts_all = bands * split
    level = group * per // per_level
    chunks = rows // piece
    tile_rows = math.gcd(SUB, piece)
    slot = send.shape[0] // n
    block = piece * groups
    forwards = band % 2 == 1
    base = share * rows

    def chunk_at(step):
        return jnp.where(forwards, step, chunks - 1 - step)

    def fetch(step, s):
        place = pl.ds(pl.multiple_of((s * rows + chunk_at(step) * piece) * groups, SUB), block)
        return pltpu.make_async_copy(x_hbm.at[place, :], x_ref.at[place, :], in_sem.at[step, s])

    for s in range(split):
        fetch(0, s).start()
    params = [
        pltpu.make_async_copy(source, target, param_sem.at[i])
        for i, (source, target) in enumerate(
            ((lon_off_hbm, lon_off), (lon_w_hbm, lon_w), (lat_off_hbm, lat_off), (lat_w_hbm, lat_w))
        )
    ]
    barrier = pltpu.get_barrier_semaphore()

    distances = sorted(range(1, n), key=lambda d: -min(d, n - d))

    def peer_at(d):
        return jnp.where(me + d >= n, me + d - n, me + d)

    for d in distances:
        pl.semaphore_signal(
            barrier, inc=1, device_id={"lon": peer_at(d)}, device_id_type=pl.DeviceIdType.MESH
        )

    def beside(step):
        other = lax.rem(part + step + parts_all, parts_all)
        return {"band": other // split, "lon": group * split + other % split}

    @pl.when(part > 0)
    def _():
        pl.semaphore_signal(
            barrier, inc=1, device_id=beside(-1), device_id_type=pl.DeviceIdType.MESH
        )

    @pl.when(part < parts_all - 1)
    def _():
        pl.semaphore_signal(
            barrier, inc=1, device_id=beside(1), device_id_type=pl.DeviceIdType.MESH
        )

    for step in range(1, chunks):
        for s in range(split):
            fetch(step, s).start()
    for param in params:
        param.start()

    def pack(step):
        for s in range(split):
            fetch(step, s).wait()

            def tile(t, carry):
                row = chunk_at(step) * piece + t * tile_rows
                start = (s * rows + row) * groups
                parts = [
                    x_ref[pl.ds(start + i, tile_rows, stride=groups), :] for i in range(groups)
                ]
                for g, part_block in enumerate(turned(parts, per)):
                    to = (g * split + s) * slot + row
                    send[pl.ds(pl.multiple_of(to, tile_rows), tile_rows), :] = part_block
                return carry

            lax.fori_loop(0, piece // tile_rows, tile, 0)

    def place_of(peer, step):
        return pl.ds(pl.multiple_of(peer * slot + chunk_at(step) * piece, SUB), piece)

    def start_all(source, target, s_sem, r_sem, step):
        place = place_of(me, step)
        pltpu.make_async_copy(source.at[place, :], target.at[place, :], r_sem.at[step]).start()
        for d in distances:
            pltpu.make_async_remote_copy(
                src_ref=source.at[place_of(peer_at(d), step), :],
                dst_ref=target.at[place, :],
                send_sem=s_sem,
                recv_sem=r_sem.at[step],
                device_id={"lon": peer_at(d)},
                device_id_type=pl.DeviceIdType.MESH,
            ).start()

    def wait_bytes(ref, sem, count):
        whole = ref.at[pl.ds(0, count), :]
        pltpu.make_async_copy(whole, whole, sem).wait()

    forward = (send, recv, send_sem, recv_sem)
    backward = (back, home, back_sem, home_sem)

    pack(0)
    above = jnp.where(part > 0, 1, 0)
    below = jnp.where(part < parts_all - 1, 1, 0)
    pl.semaphore_wait(barrier, n - 1 + above + below)
    start_all(*forward, 0)
    for step in range(1, chunks):
        pack(step)
        start_all(*forward, step)

    for param in params:
        param.wait()

    up = pltpu.make_async_remote_copy(
        src_ref=first.at[pl.ds(REACH, REACH)],
        dst_ref=halo.at[1],
        send_sem=halo_send.at[0], recv_sem=halo_recv.at[1],
        device_id=beside(-1),
        device_id_type=pl.DeviceIdType.MESH,
    )
    down = pltpu.make_async_remote_copy(
        src_ref=first.at[pl.ds(rows, REACH)],
        dst_ref=halo.at[0],
        send_sem=halo_send.at[1], recv_sem=halo_recv.at[0],
        device_id=beside(1),
        device_id_type=pl.DeviceIdType.MESH,
    )
    has_up, has_down = part > 0, part < parts_all - 1

    def send_edges(low, high):
        @pl.when(jnp.logical_and(low, has_up))
        def _():
            up.start()

        @pl.when(jnp.logical_and(high, has_down))
        def _():
            down.start()

    def take_edges(low, high):
        @pl.when(jnp.logical_and(low, has_up))
        def _():
            down.wait_recv()
            first[pl.ds(0, REACH)] = halo[0]

        @pl.when(jnp.logical_and(high, has_down))
        def _():
            up.wait_recv()
            first[pl.ds(REACH + rows, REACH)] = halo[1]

    backwards = jnp.logical_not(forwards)

    def turned_rows(places, fields, followings):
        offsets = [lon_off[level, base + row] for row in places]
        weights = [[lon_w[k, level, base + row] for k in range(4)] for row in places]
        return circled(fields, followings, offsets, weights, per, spin)

    def along(step):
        def some(t, carry):
            start = chunk_at(step) * piece + t * tile_rows
            places = [start + u for u in range(tile_rows)]
            tile = pl.multiple_of(start, tile_rows)
            recv[pl.ds(n * slot + tile, tile_rows), :] = recv[pl.ds(tile, tile_rows), :]
            fields = [recv[pl.ds(row, n, stride=slot), :] for row in places]
            followings = [recv[pl.ds(slot + row, n, stride=slot), :] for row in places]
            for row, result in zip(places, turned_rows(places, fields, followings)):
                first[REACH + row] = result
            return carry

        lax.fori_loop(0, piece // tile_rows, some, 0)

    first_row = part * rows

    def across_and_along(step):
        def some(t, carry):
            start = chunk_at(step) * piece + t * tile_rows
            places = [start + u for u in range(tile_rows)]
            fields = []
            for row in places:
                shift = lat_off[level, base + row]
                field = None
                for k in range(4):
                    source = jnp.clip(first_row + row - shift + (k - 1), 0, parts_all * rows - 1)
                    term = lat_w[k, level, base + row] * first[source - first_row + REACH]
                    field = term if field is None else field + term
                fields.append(field)
            followings = [pltpu.roll(field, n - 1, 0) for field in fields]
            for row, result in zip(places, turned_rows(places, fields, followings)):
                back[pl.ds(row, n, stride=slot), :] = result
            return carry

        lax.fori_loop(0, piece // tile_rows, some, 0)

    for step in range(chunks):
        wait_bytes(recv, recv_sem.at[step], n * piece)
        along(step)
        if chunks == 1:
            send_edges(True, True)
        elif step == 0:
            send_edges(forwards, backwards)
        elif step == chunks - 1:
            send_edges(backwards, forwards)
        if step:
            if step == 1:
                take_edges(forwards, backwards)
            across_and_along(step - 1)
            start_all(*backward, step - 1)
    if chunks == 1:
        take_edges(True, True)
    else:
        take_edges(backwards, forwards)
    across_and_along(chunks - 1)
    start_all(*backward, chunks - 1)

    for step in range(chunks):
        wait_bytes(home, home_sem.at[step], n * piece)
        for s in range(split):

            def unpack(t, carry):
                row = chunk_at(step) * piece + t * tile_rows
                start = (s * rows + row) * groups
                parts = [
                    home[pl.ds(pl.multiple_of((g * split + s) * slot + row, tile_rows), tile_rows), :]
                    for g in range(groups)
                ]
                for i, part_block in enumerate(turned(parts, per)):
                    out_ref[pl.ds(start + i, tile_rows, stride=groups), :] = part_block
                return carry

            lax.fori_loop(0, piece // tile_rows, unpack, 0)

    wait_bytes(send, send_sem, (n - 1) * rows)
    wait_bytes(back, back_sem, (n - 1) * rows)

    @pl.when(has_up)
    def _():
        up.wait_send()

    @pl.when(has_down)
    def _():
        down.wait_send()


def per_device(tracers, lon_offset, lon_weights, lat_offset, lat_weights):
    rows, width, columns = tracers.shape
    n, bands = lax.axis_size("lon"), lax.axis_size("band")
    groups = width
    per = columns // groups
    levels = lon_offset.shape[1]
    per_level = columns // levels
    split = n // groups
    assert n % groups == 0 and rows % split == 0 and per_level % per == 0
    share = rows // split
    piece = PIECE if share % PIECE == 0 else share
    chunks = share // piece
    slot = -(-share // SUB) * SUB
    flat = pltpu.VMEM((n * slot, columns), jnp.float32)
    whole = pltpu.VMEM((rows * width, columns), jnp.float32)
    dma = pltpu.SemaphoreType.DMA
    out = pl.pallas_call(
        functools.partial(kernel, n, bands, groups, share, piece, per, per_level),
        out_shape=whole,
        in_specs=[pl.BlockSpec(memory_space=pl.ANY)] * 5,
        out_specs=pl.BlockSpec(memory_space=pltpu.VMEM),
        scratch_shapes=[
            whole,
            pltpu.SMEM((levels, rows), jnp.int32),
            pltpu.SMEM((4, levels, rows), jnp.float32),
            pltpu.SMEM((levels, rows), jnp.int32),
            pltpu.SMEM((4, levels, rows), jnp.float32),
            flat,
            pltpu.VMEM(((n + 1) * slot, columns), jnp.float32),
            pltpu.VMEM((share + 2 * REACH, n, columns), jnp.float32),
            flat,
            flat,
            pltpu.VMEM((2, REACH, n, columns), jnp.float32),
            pltpu.VMEM((SUB * 2 * n, columns), jnp.float32),
            dma((chunks, split)),
            dma((4,)),
            dma,
            dma((chunks,)),
            dma,
            dma((chunks,)),
            dma((2,)),
            dma((2,)),
        ],
        compiler_params=pltpu.CompilerParams(collective_id=0, has_side_effects=True),
    )(
        tracers.reshape(rows * width, columns),
        lon_offset.T,
        lon_weights.transpose(0, 2, 1),
        lat_offset.T,
        lat_weights.transpose(0, 2, 1),
    )
    return out.reshape(rows, width, columns)


def solution(mesh):
    return jax.shard_map(
        per_device,
        mesh=mesh,
        in_specs=(
            P("band", "lon", None),
            P("band", None),
            P(None, "band", None),
            P("band", None),
            P(None, "band", None),
        ),
        out_specs=P("band", "lon", None),
        check_vma=False,
    )
```
